512 devices in a mesh: head: 8 (over x, core), ctx: 64 (over y, z).
Axes of the slice: x: 4, y: 8, z: 8, core: 2. Of those that a mesh axis runs over, the one named last changes fastest.
Arguments:
- queries: bfloat16 [512, 1024], P(None, 'head'), may hold values from -32 to 32
- keys: bfloat16 [512, 65536], P('head', 'ctx'), may hold values from -6 to 6
- values: bfloat16 [512, 65536], P('head', 'ctx'), may hold values from -6 to 6
- positions: float32 [3, 65536], P(None, 'ctx'), may hold values from 0 to 4
- falloff: float32 [8], P('head'), may hold values from 0.05 to 1
- query_ids: int32 [1024], replicated, may hold values from 0 to 65535
- cotangent: bfloat16 [512, 1024], P(None, 'head'), may hold values from -6 to 6
Outputs:
- attended: bfloat16 [512, 1024], P('head')
- query_grad: float32 [512, 1024], P('head')
- forces: float32 [3, 1024], replicated
The draws below stay inside these ranges and needn't reach their ends.
All inputs are finite; a program needn't handle non-finite values.
Results may differ from the reference program's by a relative error of at most 0.013.
Values may be sent and summed in bfloat16 or wider, within the bound.
A program may use at most 128 MiB of HBM per device.

```python
import math
import jax
import jax.numpy as jnp
from jax import lax

HEADS = 8
HEAD_DIM = 64
D = 512
NQ = 1024
NK = 65536


def draw_keys(key, part):
    sample = jnp.clip(jax.random.normal(jax.random.fold_in(key, 11), (D, NK), jnp.float32), -6.0, 6.0)
    return sample.astype(jnp.bfloat16)


def draw_queries(key, part):
    sample = jnp.clip(jax.random.normal(jax.random.fold_in(key, 12), (D, NQ), jnp.float32), -6.0, 6.0)
    return sample.astype(jnp.bfloat16)


def draw_positions(key, part):
    sample = jax.random.uniform(jax.random.fold_in(key, 13), (3, NK), jnp.float32, 0.0, 4.0)
    return sample


def with_ends(result, own_key, least, top_value):
    dims = result.shape
    index_at = [jax.random.randint(jax.random.fold_in(own_key, axis), (), 0, dims[axis]) for axis in range(len(dims))]
    result = result.at[tuple(index_at)].set(least)
    longest = dims.index(max(dims))
    index_at[longest] = (index_at[longest] + 1) % dims[longest]
    return result.at[tuple(index_at)].set(top_value)


def block_levels(stream_key, extent, pieces, smallest, largest):
    def one(dim, shards_of):
        steps = jax.random.uniform(jax.random.fold_in(jax.random.fold_in(stream_key, 6), dim), (shards_of,), jnp.float32, smallest / len(pieces), largest / len(pieces))
        return jnp.repeat(jnp.exp(steps), extent[dim] // shards_of).reshape((-1,) + (1,) * (len(extent) - dim - 1))

    gain = one(*pieces[0])
    for cut in pieces[1:]:
        gain = gain * one(*cut)
    return gain


def normal_values(rng, shape, width, most, cuts=(), kind=jnp.bfloat16):
    drawn = width * jax.random.normal(rng, shape, jnp.float32)
    if cuts:
        drawn = drawn * block_levels(rng, shape, cuts, -0.22, 0.18)
    return jnp.clip(drawn, -most, most).astype(kind)


def setup_inputs(seed: int = 0) -> dict:
    key_of = jax.random.split(jax.random.key(seed), 8)
    queries = draw_queries(jax.random.fold_in(key_of[7], 71), 0)
    keys = draw_keys(jax.random.fold_in(key_of[7], 71), 0)
    values = normal_values(key_of[2], (D, NK), 1.0, 6.0, ((0, 8), (1, 64)))
    positions = draw_positions(jax.random.fold_in(key_of[7], 71), 0)
    falloff = jnp.clip(jnp.exp(math.log(1.0) - 2.9957323 * jax.random.uniform(key_of[4], (HEADS,), jnp.float32) ** block_levels(key_of[4], (HEADS,), ((0, 8),), -0.2, 0.2)), 0.05, 1.0)
    query_ids = with_ends(jax.random.randint(key_of[5], (NQ,), 0, NK), jax.random.fold_in(key_of[5], 1), 0, NK - 1).astype(jnp.int32)
    cotangent = normal_values(key_of[6], (D, NQ), 1.0, 6.0, ((1, 8),))
    return {"queries": queries, "keys": keys, "values": values, "positions": positions, "falloff": falloff, "query_ids": query_ids, "cotangent": cotangent}


def reference(queries, keys, values, positions, falloff, query_ids, cotangent):
    scaling = HEAD_DIM ** -0.5
    key_block = math.gcd(NK, 4096)
    block_count = NK // key_block
    query_place = jnp.take(positions, query_ids, axis=1)
    query_heads = queries.astype(jnp.float32).reshape(HEADS, HEAD_DIM, NQ)
    grad_heads = cotangent.astype(jnp.float32).reshape(HEADS, HEAD_DIM, NQ)
    keys_wide = keys.astype(jnp.float32)
    values_wide = values.astype(jnp.float32)

    def block_parts(index):
        offset = index * key_block
        key_heads = lax.dynamic_slice_in_dim(keys_wide, offset, key_block, 1).reshape(HEADS, HEAD_DIM, key_block)
        value_heads = lax.dynamic_slice_in_dim(values_wide, offset, key_block, 1).reshape(HEADS, HEAD_DIM, key_block)
        place_part = lax.dynamic_slice_in_dim(positions, offset, key_block, 1)
        dots = jnp.einsum('hcq,hck->hqk', query_heads, key_heads) * scaling
        dist = jnp.zeros((NQ, key_block), jnp.float32)
        for axis_id in range(3):
            gap = query_place[axis_id][:, None] - place_part[axis_id][None, :]
            dist = dist + gap * gap
        scores = dots - falloff[:, None, None] * dist[None]
        return scores, key_heads, value_heads, place_part

    def forward_step(carry, index):
        run_max, run_total, accum = carry
        scores, key_heads, value_heads, place_part = block_parts(index)
        new_max = jnp.maximum(run_max, jnp.max(scores, axis=-1))
        shrink = jnp.exp(run_max - new_max)
        weights = jnp.exp(scores - new_max[..., None])
        low = lax.optimization_barrier(weights.astype(jnp.bfloat16)).astype(jnp.float32)
        accum = accum * shrink[:, None, :] + jnp.einsum('hck,hqk->hcq', value_heads, low)
        run_total = run_total * shrink + jnp.sum(weights, axis=-1)
        return (new_max, run_total, accum), None

    start = (jnp.full((HEADS, NQ), -jnp.inf, jnp.float32), jnp.zeros((HEADS, NQ), jnp.float32),
             jnp.zeros((HEADS, HEAD_DIM, NQ), jnp.float32))
    (row_max, row_total, accum), _ = lax.scan(forward_step, start, jnp.arange(block_count, dtype=jnp.int32))
    output32 = accum / row_total[:, None, :]
    attended = output32.reshape(D, NQ).astype(jnp.bfloat16)
    log_total = row_max + jnp.log(row_total)
    row_delta = jnp.sum(grad_heads * output32, axis=1)

    def backward_step(carry, index):
        query_grad, force_sum = carry
        scores, key_heads, value_heads, place_part = block_parts(index)
        probs = jnp.exp(scores - log_total[..., None])
        grad_probs = jnp.einsum('hcq,hck->hqk', grad_heads, value_heads)
        grad_scores = probs * (grad_probs - row_delta[..., None])
        low = lax.optimization_barrier(grad_scores.astype(jnp.bfloat16)).astype(jnp.float32)
        query_grad = query_grad + jnp.einsum('hck,hqk->hcq', key_heads, low) * scaling
        pull = jnp.sum(2.0 * falloff[:, None, None] * grad_scores, axis=0)
        toward = lax.dot_general(place_part, pull, (((1,), (1,)), ((), ())), precision=lax.Precision.HIGHEST)
        force_sum = force_sum - query_place * jnp.sum(pull, axis=-1)[None, :] + toward
        return (query_grad, force_sum), None

    start = (jnp.zeros((HEADS, HEAD_DIM, NQ), jnp.float32), jnp.zeros((3, NQ), jnp.float32))
    (query_grad, forces), _ = lax.scan(backward_step, start, jnp.arange(block_count, dtype=jnp.int32))
    return attended, query_grad.reshape(D, NQ), forces
```

```python
import functools

import jax
import jax.numpy as jnp
from jax import lax
from jax.experimental import pallas as pl
from jax.experimental.pallas import tpu as pltpu
from jax.sharding import PartitionSpec as P

MESH = pl.DeviceIdType.MESH
HEAD_DIM = 64
SIDE = 8
LANES = 128
CENTER = 2.0
F32 = jnp.float32
BF16 = jnp.bfloat16


def dot(a, b):
    return jnp.dot(a, b, preferred_element_type=F32)


def pieces(x, count):
    out = []
    for _ in range(count):
        part = x.astype(BF16).astype(F32)
        out.append(part)
        x = x - part
    return out


def rows(shape):
    return lax.broadcasted_iota(jnp.int32, shape, 0)


def merge(stats, parts):
    logs = [s[3:4] for s in stats]
    deltas = [s[7:8] for s in stats]
    top = functools.reduce(jnp.maximum, logs)
    weights = [jnp.exp(x - top) for x in logs]
    total = functools.reduce(jnp.add, weights)
    inverse = 1.0 / total
    weights = [w * inverse for w in weights]
    delta = functools.reduce(jnp.add, [w * d for w, d in zip(weights, deltas)])
    shifts = [w * (d - delta) for w, d in zip(weights, deltas)]
    plain = functools.reduce(jnp.add, [w * s for w, s in zip(weights, stats)])
    moved = functools.reduce(
        jnp.add, [t * pltpu.roll(s, 4, 0) for t, s in zip(shifts, stats)]
    )
    at = rows(plain.shape)
    stat = jnp.where(
        at < 3,
        plain + moved,
        jnp.where(at == 3, top + jnp.log(total), jnp.where(at < 7, plain, delta)),
    )
    a = b = c = None
    for i, (w, t) in enumerate(zip(weights, shifts)):
        ai, bi, ci = parts(i)
        ai, bi, ci = w * ai, w * bi + t * ci, w * ci
        a, b, c = (ai, bi, ci) if a is None else (a + ai, b + bi, c + ci)
    return a, b, c, stat


def kernel(
    q_hbm, k_hbm, v_hbm, pos_ref, fall_ref, ids_ref, g_hbm,
    att_ref, qg_ref, f_ref,
    left, kt, vt, xs, qin, gin, qx, pick1, pick2, pick3, s_buf, p_buf, dp_buf,
    part_buf, stat_buf, sb2, rb2, gath, fin, fgath,
    local_sem, send, recv,
):
    h, ctx = lax.axis_index("head"), lax.axis_index("ctx")
    parity = h % 2
    y, z = ctx // SIDE, ctx % SIDE
    m1, m2 = SIDE - (SIDE - 1) * parity, 1 + (SIDE - 1) * parity
    a1 = y + parity * (z - y)
    a2 = z + parity * (y - z)

    def peer1(o):
        b = (a1 + o) % SIDE
        return (h, b * m1 + a2 * m2)

    def peer2(o):
        b = (a2 + o) % SIDE
        return (h, a1 * m1 + b * m2)

    def peerh(o):
        return ((h + o) % SIDE, ctx)

    def peerf(o):
        other = (h + o) % SIDE
        odd = (other + h) % 2
        flipped = z * SIDE + y
        return (other, ctx + odd * (flipped - ctx))

    def copy(phase, o, src, dst, dev):
        return pltpu.make_async_remote_copy(
            src_ref=src, dst_ref=dst, send_sem=send.at[phase, o],
            recv_sem=recv.at[phase, o], device_id=dev, device_id_type=MESH,
        )

    def loop(body):
        def step(o, carry):
            body(o)
            return carry
        lax.fori_loop(1, SIDE, step, 0)

    load_v = pltpu.make_async_copy(v_hbm, left.at[pl.ds(0, 64)], local_sem.at[0])
    load_k = pltpu.make_async_copy(k_hbm, left.at[pl.ds(64, 64)], local_sem.at[1])
    own_rows = pl.ds(pl.multiple_of(h * HEAD_DIM, HEAD_DIM), HEAD_DIM)
    load_q = pltpu.make_async_copy(q_hbm.at[own_rows], qin.at[h], local_sem.at[2])
    load_g = pltpu.make_async_copy(g_hbm.at[own_rows], gin.at[h], local_sem.at[3])
    load_v.start()
    load_k.start()
    load_q.start()
    load_g.start()

    barrier = pltpu.get_barrier_semaphore()

    def greet(o):
        for dev in (peer1(o), peer2(o), peerh(o), peerf(o)):
            pl.semaphore_signal(barrier, inc=1, device_id=dev, device_id_type=MESH)

    loop(greet)

    place = pos_ref[...] - CENTER
    falloff = fall_ref[0]
    xs[0:3, :] = place
    xs[3:4, :] = -falloff * jnp.sum(place * place, axis=0, keepdims=True)
    xs[4:7, :] = place
    xs[7:8, :] = jnp.ones((1, place.shape[1]), F32)
    x1, x2, x3 = pieces(xs[...], 3)
    keys_at = jnp.concatenate([x1, x2, x3, x1], axis=0).astype(BF16)
    left[128:144, :] = jnp.concatenate([x1, x2], axis=0).astype(BF16)
    key_count = place.shape[1]
    local = ids_ref[pl.ds(h, 1), :] - ctx * key_count
    hot = (rows((key_count, LANES)) == local).astype(F32).astype(BF16)
    found = dot(keys_at, hot)
    pick1[a1] = found[0:8] + found[8:16] + found[16:24]

    pl.semaphore_wait(barrier, 4 * (SIDE - 1))

    loop(lambda o: copy(0, o, pick1.at[a1], pick1.at[a1], peer1(o)).start())

    def send_rows(o):
        other, _ = peerh(o)
        part = pl.ds(pl.multiple_of(other * HEAD_DIM, HEAD_DIM), HEAD_DIM)
        copy(1, o, g_hbm.at[part], gin.at[h], peerh(o)).start()
        copy(2, o, q_hbm.at[part], qin.at[h], peerh(o)).start()

    loop(send_rows)

    load_k.wait()
    load_v.wait()
    kt[...] = jnp.concatenate([left[64:128, :], keys_at], axis=0).T
    vt[...] = left[0:64, :].T
    load_q.wait()
    load_g.wait()

    def source(o, me):
        return (me + SIDE - o) % SIDE

    loop(lambda o: copy(0, o, pick1.at[a1], pick1.at[source(o, a1)], peer1(o)).wait_recv())
    pick2[a2] = functools.reduce(jnp.add, [pick1[i] for i in range(SIDE)])
    loop(lambda o: copy(3, o, pick2.at[a2], pick2.at[a2], peer2(o)).start())

    def wait_g(o):
        copy(1, o, gin.at[h], gin.at[source(o, h)], peerh(o)).wait_recv()

    def wait_q(o):
        copy(2, o, qin.at[h], qin.at[source(o, h)], peerh(o)).wait_recv()

    loop(wait_g)

    def chunk(o):
        return (a1 + o) % SIDE

    def grads(t):
        cot = jnp.concatenate([gin[chunk(2 * t + 1)], gin[chunk(2 * t + 2)]], axis=1)
        dp_buf[t] = dot(vt[...], cot)

    def grad_step(t, carry):
        grads(t)
        return carry

    lax.fori_loop(0, 2, grad_step, 0)
    loop(lambda o: copy(3, o, pick2.at[a2], pick2.at[source(o, a2)], peer2(o)).wait_recv())
    pick3[h] = functools.reduce(jnp.add, [pick2[i] for i in range(SIDE)])
    loop(lambda o: copy(4, o, pick3.at[h], pick3.at[h], peerh(o)).start())
    lax.fori_loop(2, 4, grad_step, 0)
    loop(wait_q)
    loop(lambda o: copy(4, o, pick3.at[h], pick3.at[source(o, h)], peerh(o)).wait_recv())

    def build(c, carry):
        spot = pick3[c]
        at = rows(spot.shape)
        side = jnp.where(at < 3, (2.0 * falloff) * spot, jnp.where(at == 3, 1.0, 0.0))
        t1, t2 = pieces(side, 2)
        qx[c, 0:64, :] = qin[c] * jnp.asarray(HEAD_DIM ** -0.5, BF16)
        qx[c, 64:96, :] = jnp.concatenate([t1, t1, t1, t2], axis=0).astype(BF16)
        return carry

    lax.fori_loop(0, SIDE, build, 0)

    blocks = [pl.ds(i * 256, 256) for i in range(key_count // 256)]

    def attend(t, carry):
        chunks = [chunk(2 * t + 1), chunk(2 * t + 2)]
        q = jnp.concatenate([qx[c] for c in chunks], axis=1)
        cot = jnp.concatenate([gin[c] for c in chunks], axis=1).astype(F32)
        top = None
        for part in blocks:
            s = dot(kt[part, :], q)
            s_buf[part, :] = s
            m = jnp.max(s, axis=0, keepdims=True)
            top = m if top is None else jnp.maximum(top, m)
        for part in blocks:
            p = jnp.exp(s_buf[part, :] - top)
            s_buf[part, :] = p
            p_buf[part, :] = p.astype(BF16)
        r = dot(left[...], p_buf[...])
        total = r[135:136]
        inverse = 1.0 / total
        a = r[0:64] * inverse
        c = r[64:128] * inverse
        px = (r[128:136] + r[136:144]) * inverse
        delta = jnp.sum(a * cot, axis=0, keepdims=True)
        for part in blocks:
            w = s_buf[part, :] * (dp_buf[t, part, :] - delta)
            p_buf[part, :] = w.astype(BF16)
        r = dot(left[64:144, :], p_buf[...])
        b = r[0:64] * inverse
        wx = (r[64:72] + r[72:80]) * inverse
        spot = jnp.concatenate([pick3[c] for c in chunks], axis=1)
        at = rows(spot.shape)
        stat = jnp.where(
            at < 3,
            wx - spot * wx[7:8],
            jnp.where(
                at == 3,
                top + jnp.log(total),
                jnp.where(at < 7, px - spot * px[7:8], delta),
            ),
        )
        for i in range(2):
            o = (2 * t + 1 + i) % SIDE
            slot = jnp.where(o == 0, a1, SIDE + o)
            lanes = slice(i * LANES, (i + 1) * LANES)
            part_buf[slot, 0:64, :] = a[:, lanes].astype(BF16)
            part_buf[slot, 64:128, :] = b[:, lanes].astype(BF16)
            part_buf[slot, 128:192, :] = c[:, lanes].astype(BF16)
            stat_buf[slot] = stat[:, lanes]

            @pl.when(o != 0)
            def _():
                copy(5, o, part_buf.at[slot], part_buf.at[a1], peer1(o)).start()
                copy(6, o, stat_buf.at[slot], stat_buf.at[a1], peer1(o)).start()

        return carry

    lax.fori_loop(0, SIDE // 2, attend, 0)

    def wait_parts(o):
        copy(5, o, part_buf.at[SIDE + o], part_buf.at[source(o, a1)], peer1(o)).wait_recv()
        copy(6, o, stat_buf.at[SIDE + o], stat_buf.at[source(o, a1)], peer1(o)).wait_recv()

    loop(wait_parts)

    def parts1(i):
        x = part_buf[i].astype(F32)
        return x[0:64], x[64:128], x[128:192]

    a, b, c, stat = merge([stat_buf[i] for i in range(SIDE)], parts1)
    for j in range(SIDE):
        part = slice(8 * j, 8 * j + 8)
        sb2[j, 0:8, :] = a[part]
        sb2[j, 8:16, :] = b[part]
        sb2[j, 16:24, :] = c[part]
        sb2[j, 24:32, :] = stat
    rb2[a2] = sb2[a2]

    def send_second(o):
        copy(7, o, sb2.at[(a2 + o) % SIDE], rb2.at[a2], peer2(o)).start()

    loop(send_second)
    loop(lambda o: copy(7, o, sb2.at[0], rb2.at[source(o, a2)], peer2(o)).wait_recv())

    def parts2(i):
        x = rb2[i]
        return x[0:8], x[8:16], x[16:24]

    a, b, c, stat = merge([rb2[i, 24:32, :] for i in range(SIDE)], parts2)
    gath[a1, a2] = jnp.concatenate([a, b * HEAD_DIM ** -0.5], axis=0).astype(BF16)
    fin[h] = (2.0 * falloff) * stat
    loop(lambda o: copy(8, o, gath.at[a1, a2], gath.at[a1, a2], peer2(o)).start())
    loop(lambda o: copy(9, o, fin.at[h], fin.at[h], peerf(o)).start())
    loop(lambda o: copy(8, o, gath.at[a1, a2], gath.at[a1, source(o, a2)], peer2(o)).wait_recv())
    loop(lambda o: copy(10, o, gath.at[a1], gath.at[a1], peer1(o)).start())
    loop(lambda o: copy(9, o, fin.at[h], fin.at[source(o, h)], peerf(o)).wait_recv())
    fgath[a1] = functools.reduce(jnp.add, [fin[i] for i in range(SIDE)])
    loop(lambda o: copy(11, o, fgath.at[a1], fgath.at[a1], peer1(o)).start())

    loop(lambda o: copy(10, o, gath.at[a1], gath.at[source(o, a1)], peer1(o)).wait_recv())
    for i in range(SIDE):
        lanes = slice(i * LANES, (i + 1) * LANES)
        for j in range(0, SIDE, 2):
            lo, hi = gath[i, j].astype(F32), gath[i, j + 1].astype(F32)
            att_ref[8 * j:8 * j + 16, lanes] = jnp.concatenate([lo[0:8], hi[0:8]], axis=0).astype(BF16)
            qg_ref[8 * j:8 * j + 8, lanes] = lo[8:16]
            qg_ref[8 * j + 8:8 * j + 16, lanes] = hi[8:16]
    loop(lambda o: copy(11, o, fgath.at[a1], fgath.at[source(o, a1)], peer1(o)).wait_recv())
    for i in range(SIDE):
        f_ref[:, i * LANES:(i + 1) * LANES] = fgath[i, 0:3, :]

    def drain(o):
        copy(0, o, pick1.at[a1], pick1.at[a1], peer1(o)).wait_send()
        copy(1, o, gin.at[h], gin.at[h], peerh(o)).wait_send()
        copy(2, o, qin.at[h], qin.at[h], peerh(o)).wait_send()
        copy(3, o, pick2.at[a2], pick2.at[a2], peer2(o)).wait_send()
        copy(4, o, pick3.at[h], pick3.at[h], peerh(o)).wait_send()
        copy(5, o, part_buf.at[SIDE + o], part_buf.at[a1], peer1(o)).wait_send()
        copy(6, o, stat_buf.at[SIDE + o], stat_buf.at[a1], peer1(o)).wait_send()
        copy(7, o, sb2.at[0], rb2.at[a2], peer2(o)).wait_send()
        copy(8, o, gath.at[a1, a2], gath.at[a1, a2], peer2(o)).wait_send()
        copy(9, o, fin.at[h], fin.at[h], peerf(o)).wait_send()
        copy(10, o, gath.at[a1], gath.at[a1], peer1(o)).wait_send()
        copy(11, o, fgath.at[a1], fgath.at[a1], peer1(o)).wait_send()

    loop(drain)


def shards(queries, keys, values, positions, falloff, query_ids, cotangent):
    nk = keys.shape[1]
    nq = query_ids.shape[0]
    ids = query_ids.reshape(SIDE, LANES)
    vmem = pl.BlockSpec(memory_space=pltpu.VMEM)
    smem = pl.BlockSpec(memory_space=pltpu.SMEM)
    any_ = pl.BlockSpec(memory_space=pl.ANY)
    return pl.pallas_call(
        kernel,
        out_shape=(
            jax.ShapeDtypeStruct((HEAD_DIM, nq), BF16),
            jax.ShapeDtypeStruct((HEAD_DIM, nq), F32),
            jax.ShapeDtypeStruct((3, nq), F32),
        ),
        in_specs=[any_, any_, any_, vmem, smem, vmem, any_],
        out_specs=(vmem, vmem, vmem),
        scratch_shapes=[
            pltpu.VMEM((144, nk), BF16),
            pltpu.VMEM((nk, 96), BF16),
            pltpu.VMEM((nk, 64), BF16),
            pltpu.VMEM((8, nk), F32),
            pltpu.VMEM((SIDE, HEAD_DIM, LANES), BF16),
            pltpu.VMEM((SIDE, HEAD_DIM, LANES), BF16),
            pltpu.VMEM((SIDE, 96, LANES), BF16),
            pltpu.VMEM((SIDE, 8, LANES), F32),
            pltpu.VMEM((SIDE, 8, LANES), F32),
            pltpu.VMEM((SIDE, 8, LANES), F32),
            pltpu.VMEM((nk, 2 * LANES), F32),
            pltpu.VMEM((nk, 2 * LANES), BF16),
            pltpu.VMEM((SIDE // 2, nk, 2 * LANES), F32),
            pltpu.VMEM((2 * SIDE, 192, LANES), BF16),
            pltpu.VMEM((2 * SIDE, 8, LANES), F32),
            pltpu.VMEM((SIDE, 32, LANES), F32),
            pltpu.VMEM((SIDE, 32, LANES), F32),
            pltpu.VMEM((SIDE, SIDE, 16, LANES), BF16),
            pltpu.VMEM((SIDE, 8, LANES), F32),
            pltpu.VMEM((SIDE, 8, LANES), F32),
            pltpu.SemaphoreType.DMA((4,)),
            pltpu.SemaphoreType.DMA((12, SIDE)),
            pltpu.SemaphoreType.DMA((12, SIDE)),
        ],
        compiler_params=pltpu.CompilerParams(
            collective_id=0, has_side_effects=True, vmem_limit_bytes=40 * 1024 * 1024
        ),
    )(queries, keys, values, positions, falloff, ids, cotangent)


def solution(mesh):
    return jax.shard_map(
        shards,
        mesh=mesh,
        in_specs=(
            P(None, "head"),
            P("head", "ctx"),
            P("head", "ctx"),
            P(None, "ctx"),
            P("head"),
            P(),
            P(None, "head"),
        ),
        out_specs=(P("head", None), P("head", None), P()),
        check_vma=False,
    )
```

```python
import functools

import jax
import jax.numpy as jnp
from jax import lax
from jax.experimental import pallas as pl
from jax.experimental.pallas import tpu as pltpu
from jax.sharding import PartitionSpec as P

MESH = pl.DeviceIdType.MESH
HEAD_DIM = 64
SIDE = 8
LANES = 128
CENTER = 2.0
F32 = jnp.float32
BF16 = jnp.bfloat16


def dot(a, b):
    return jnp.dot(a, b, preferred_element_type=F32)


def pieces(x, count):
    out = []
    for _ in range(count):
        part = x.astype(BF16).astype(F32)
        out.append(part)
        x = x - part
    return out


def rows(shape):
    return lax.broadcasted_iota(jnp.int32, shape, 0)


def merge(stats, parts):
    logs = [s[3:4] for s in stats]
    deltas = [s[7:8] for s in stats]
    top = functools.reduce(jnp.maximum, logs)
    weights = [jnp.exp(x - top) for x in logs]
    total = functools.reduce(jnp.add, weights)
    inverse = 1.0 / total
    weights = [w * inverse for w in weights]
    delta = functools.reduce(jnp.add, [w * d for w, d in zip(weights, deltas)])
    shifts = [w * (d - delta) for w, d in zip(weights, deltas)]
    plain = functools.reduce(jnp.add, [w * s for w, s in zip(weights, stats)])
    moved = functools.reduce(
        jnp.add, [t * pltpu.roll(s, 4, 0) for t, s in zip(shifts, stats)]
    )
    at = rows(plain.shape)
    stat = jnp.where(
        at < 3,
        plain + moved,
        jnp.where(at == 3, top + jnp.log(total), jnp.where(at < 7, plain, delta)),
    )
    a = b = c = None
    for i, (w, t) in enumerate(zip(weights, shifts)):
        ai, bi, ci = parts(i)
        ai, bi, ci = w * ai, w * bi + t * ci, w * ci
        a, b, c = (ai, bi, ci) if a is None else (a + ai, b + bi, c + ci)
    return a, b, c, stat


def kernel(
    q_hbm, k_hbm, v_hbm, pos_hbm, fall_hbm, ids_hbm, g_hbm,
    att_ref, qg_ref, f_ref,
    pos, fall, ids, left, kt, vt, xs, qin, gin, qx, pick1, pick2, pick3, s_buf, p_buf,
    dp_buf, part_buf, stat_buf, sb2, rb2, gath, fin, fgath,
    local_sem, send, recv,
):
    h, ctx = lax.axis_index("head"), lax.axis_index("ctx")
    parity = h % 2
    mate = h + 1 - 2 * parity
    y, z = ctx // SIDE, ctx % SIDE
    m1, m2 = SIDE - (SIDE - 1) * parity, 1 + (SIDE - 1) * parity
    a1 = y + parity * (z - y)
    a2 = z + parity * (y - z)

    def on1(o):
        return ((a1 + o) % SIDE) * m1 + a2 * m2

    def on2(o):
        return a1 * m1 + ((a2 + o) % SIDE) * m2

    def far(k):
        return (SIDE // 2 + (1 - 2 * (k % 2)) * ((k + 1) // 2)) % SIDE

    def copy(phase, src, dst, dev):
        return pltpu.make_async_remote_copy(
            src_ref=src, dst_ref=dst, send_sem=send.at[phase],
            recv_sem=recv.at[phase], device_id=dev, device_id_type=MESH,
        )

    def loop(count, body):
        def step(o, carry):
            body(o)
            return carry
        lax.fori_loop(0, count, step, 0)

    def arrived(phase, ref):
        copy(phase, ref, ref, (h, ctx)).wait_recv()

    def sent(phase, ref):
        copy(phase, ref, ref, (h, ctx)).wait_send()

    def seven(ref):
        return ref.at[pl.ds(0, SIDE - 1)]

    own_rows = pl.ds(pl.multiple_of(h * HEAD_DIM, HEAD_DIM), HEAD_DIM)
    loads = [
        pltpu.make_async_copy(src, dst, local_sem.at[i])
        for i, (src, dst) in enumerate([
            (pos_hbm, pos), (fall_hbm, fall), (ids_hbm, ids),
            (k_hbm, left.at[pl.ds(64, 64)]), (v_hbm, left.at[pl.ds(0, 64)]),
            (g_hbm.at[own_rows], gin.at[h]), (q_hbm.at[own_rows], qin.at[h]),
        ])
    ]
    for load in loads[:3]:
        load.start()

    barrier = pltpu.get_barrier_semaphore()

    def greet(head, at):
        pl.semaphore_signal(barrier, inc=1, device_id=(head, at), device_id_type=MESH)

    def greet_seven(k):
        o = far(k)
        greet(h, on1(o))
        greet(h, on2(o))
        greet((h + o) % SIDE, ctx)

    loop(SIDE - 1, greet_seven)
    loop(SIDE, lambda k: greet(mate, on1(far(k))))

    for load in loads[3:]:
        load.start()
    for load in loads[:3]:
        load.wait()
    place = pos[...] - CENTER
    key_count = place.shape[1]
    falloff = fall[...]
    xs[0:3, :] = place
    xs[3:4, :] = -falloff * jnp.sum(place * place, axis=0, keepdims=True)
    xs[4:7, :] = place
    xs[7:8, :] = jnp.ones((1, key_count), F32)
    x1, x2, x3 = pieces(xs[...], 3)
    keys_at = jnp.concatenate([x1, x2, x3, x1], axis=0).astype(BF16)
    for half in range(2):
        tiles = []
        for i in range(2):
            local = ids[pl.ds(4 * parity + 2 * half + i, 1), :] - ctx * key_count
            hot = (rows((key_count, LANES)) == local).astype(F32).astype(BF16)
            found = dot(keys_at[0:24], hot)
            tiles.append(found[0:8] + found[8:16] + found[16:24])
        pick1[a1, half] = jnp.where(rows(tiles[0].shape) < 4, tiles[0], tiles[1])
    pl.semaphore_wait(barrier, 3 * (SIDE - 1) + SIDE)
    loop(SIDE - 1, lambda k: copy(0, pick1.at[a1], pick1.at[a1], (h, on1(far(k)))).start())

    def send_rows(ref_hbm, ref, phase):
        def body(k):
            other = (h + far(k)) % SIDE
            part = pl.ds(pl.multiple_of(other * HEAD_DIM, HEAD_DIM), HEAD_DIM)
            copy(phase, ref_hbm.at[part], ref.at[h], (other, ctx)).start()
        loop(SIDE - 1, body)

    send_rows(g_hbm, gin, 1)
    send_rows(q_hbm, qin, 2)
    for load in loads[3:]:
        load.wait()
    left[128:144, :] = jnp.concatenate([x1, x2], axis=0).astype(BF16)
    kt[...] = jnp.concatenate([left[64:128, :], keys_at], axis=0).T
    vt[...] = left[0:64, :].T
    arrived(0, seven(pick1))
    pick2[SIDE * parity + a2] = functools.reduce(jnp.add, [pick1[i] for i in range(SIDE)])
    mine = pick2.at[SIDE * parity + a2]
    loop(SIDE - 1, lambda k: copy(3, mine, mine, (h, on2(far(k)))).start())
    loop(SIDE, lambda k: copy(3, mine, mine, (mate, on2(far(k)))).start())
    arrived(1, seven(gin))

    def chunks(t):
        return [(a1 + SIDE // 2 - t) % SIDE, (a1 + SIDE // 2 + 1 + t) % SIDE]

    def grads(t):
        cot = jnp.concatenate([gin[c] for c in chunks(t)], axis=1)
        dp_buf[t] = dot(vt[...], cot)

    loop(SIDE // 2, grads)
    arrived(2, seven(qin))
    arrived(3, pick2.at[pl.ds(0, 2 * SIDE - 1)])
    for p in range(2):
        pairs = functools.reduce(jnp.add, [pick2[SIDE * p + i] for i in range(SIDE)])
        for half in range(2):
            pair = pairs[half]
            low = rows(pair.shape) < 4
            swapped = pltpu.roll(pair, 4, 0)
            pick3[4 * p + 2 * half] = jnp.where(low, pair, swapped)
            pick3[4 * p + 2 * half + 1] = jnp.where(low, swapped, pair)

    def build(c):
        spot = pick3[c]
        at = rows(spot.shape)
        side = jnp.where(at < 3, (2.0 * falloff) * spot, jnp.where(at == 3, 1.0, 0.0))
        t1, t2 = pieces(side, 2)
        qx[c, 0:64, :] = qin[c] * jnp.asarray(HEAD_DIM ** -0.5, BF16)
        qx[c, 64:96, :] = jnp.concatenate([t1, t1, t1, t2], axis=0).astype(BF16)

    loop(SIDE, build)

    blocks = [pl.ds(i * 256, 256) for i in range(key_count // 256)]

    def attend(t):
        mine = chunks(t)
        q = jnp.concatenate([qx[c] for c in mine], axis=1)
        cot = jnp.concatenate([gin[c] for c in mine], axis=1).astype(F32)
        top = None
        for part in blocks:
            s = dot(kt[part, :], q)
            s_buf[part, :] = s
            m = jnp.max(s, axis=0, keepdims=True)
            top = m if top is None else jnp.maximum(top, m)
        for part in blocks:
            p = jnp.exp(s_buf[part, :] - top)
            s_buf[part, :] = p
            p_buf[part, :] = p.astype(BF16)
        r = dot(left[...], p_buf[...])
        total = r[135:136]
        inverse = 1.0 / total
        a = r[0:64] * inverse
        c = r[64:128] * inverse
        px = (r[128:136] + r[136:144]) * inverse
        delta = jnp.sum(a * cot, axis=0, keepdims=True)
        for part in blocks:
            w = s_buf[part, :] * (dp_buf[t, part, :] - delta)
            p_buf[part, :] = w.astype(BF16)
        r = dot(left[64:144, :], p_buf[...])
        b = r[0:64] * inverse
        wx = (r[64:72] + r[72:80]) * inverse
        spot = jnp.concatenate([pick3[c] for c in mine], axis=1)
        at = rows(spot.shape)
        stat = jnp.where(
            at < 3,
            wx - spot * wx[7:8],
            jnp.where(
                at == 3,
                top + jnp.log(total),
                jnp.where(at < 7, px - spot * px[7:8], delta),
            ),
        )
        for i in range(2):
            o = (mine[i] + SIDE - a1) % SIDE
            slot = jnp.where(o == 0, a1, SIDE + o)
            lanes = slice(i * LANES, (i + 1) * LANES)
            part_buf[slot, 0:64, :] = a[:, lanes].astype(BF16)
            part_buf[slot, 64:128, :] = b[:, lanes].astype(BF16)
            part_buf[slot, 128:192, :] = c[:, lanes].astype(BF16)
            stat_buf[slot] = stat[:, lanes]

            @pl.when(o != 0)
            def _():
                copy(4, part_buf.at[slot], part_buf.at[a1], (h, on1(o))).start()
                copy(5, stat_buf.at[slot], stat_buf.at[a1], (h, on1(o))).start()

    loop(SIDE // 2, attend)
    arrived(5, seven(stat_buf))
    arrived(4, seven(part_buf))
    def parts1(i):
        x = part_buf[i].astype(F32)
        return x[0:64], x[64:128], x[128:192]

    a, b, c, stat = merge([stat_buf[i] for i in range(SIDE)], parts1)
    for j in range(SIDE):
        part = slice(8 * j, 8 * j + 8)
        sb2[j, 0:8, :] = a[part]
        sb2[j, 8:16, :] = b[part]
        sb2[j, 16:24, :] = c[part]
        sb2[j, 24:32, :] = stat
    def send_second(k):
        o = far(k)
        copy(6, sb2.at[(a2 + o) % SIDE], rb2.at[a2], (h, on2(o))).start()

    loop(SIDE - 1, send_second)
    rb2[a2] = sb2[a2]
    arrived(6, seven(rb2))
    def parts2(i):
        x = rb2[i]
        return x[0:8], x[8:16], x[16:24]

    a, b, c, stat = merge([rb2[i, 24:32, :] for i in range(SIDE)], parts2)
    fin[h // 2] = (2.0 * falloff) * stat
    tile = SIDE * a1 + a2
    gath[tile] = jnp.concatenate([a, b * HEAD_DIM ** -0.5], axis=0).astype(BF16)
    def send_force(k):
        other = (h + 2 + 2 * k) % SIDE
        copy(7, fin.at[h // 2], fin.at[h // 2], (other, ctx)).start()

    loop(3, send_force)

    def send_tile(k1, k2):
        at = ((a1 + far(k1)) % SIDE) * m1 + ((a2 + far(k2)) % SIDE) * m2
        copy(8, gath.at[tile], gath.at[tile], (h, at)).start()

    loop(SIDE * (SIDE - 1), lambda k: send_tile(k // SIDE, k % SIDE))
    loop(SIDE - 1, lambda k: send_tile(SIDE - 1, k))
    arrived(7, fin.at[pl.ds(0, 3)])
    fgath[SIDE * parity + a1] = functools.reduce(jnp.add, [fin[i] for i in range(4)])
    ours = fgath.at[SIDE * parity + a1]
    loop(SIDE - 1, lambda k: copy(9, ours, ours, (h, on1(far(k)))).start())
    loop(SIDE, lambda k: copy(9, ours, ours, (mate, on1(far(k)))).start())
    arrived(8, gath.at[pl.ds(0, SIDE * SIDE - 1)])
    for i in range(SIDE):
        lanes = slice(i * LANES, (i + 1) * LANES)
        for j in range(0, SIDE, 2):
            lo, hi = gath[SIDE * i + j].astype(F32), gath[SIDE * i + j + 1].astype(F32)
            att_ref[8 * j:8 * j + 16, lanes] = jnp.concatenate([lo[0:8], hi[0:8]], axis=0).astype(BF16)
            qg_ref[8 * j:8 * j + 8, lanes] = lo[8:16]
            qg_ref[8 * j + 8:8 * j + 16, lanes] = hi[8:16]
    arrived(9, fgath.at[pl.ds(0, 2 * SIDE - 1)])
    for i in range(SIDE):
        f_ref[:, i * LANES:(i + 1) * LANES] = fgath[i, 0:3, :] + fgath[SIDE + i, 0:3, :]
    sent(0, seven(pick1))
    sent(1, seven(gin))
    sent(2, seven(qin))
    sent(3, pick2.at[pl.ds(0, 2 * SIDE - 1)])
    sent(4, seven(part_buf))
    sent(5, seven(stat_buf))
    sent(6, seven(rb2))
    sent(7, fin.at[pl.ds(0, 3)])
    sent(8, gath.at[pl.ds(0, SIDE * SIDE - 1)])
    sent(9, fgath.at[pl.ds(0, 2 * SIDE - 1)])


def shards(queries, keys, values, positions, falloff, query_ids, cotangent):
    nk = keys.shape[1]
    nq = query_ids.shape[0]
    ids = query_ids.reshape(SIDE, LANES)
    vmem = pl.BlockSpec(memory_space=pltpu.VMEM)
    any_ = pl.BlockSpec(memory_space=pl.ANY)
    return pl.pallas_call(
        kernel,
        out_shape=(
            jax.ShapeDtypeStruct((HEAD_DIM, nq), BF16),
            jax.ShapeDtypeStruct((HEAD_DIM, nq), F32),
            jax.ShapeDtypeStruct((3, nq), F32),
        ),
        in_specs=[any_] * 7,
        out_specs=(vmem, vmem, vmem),
        scratch_shapes=[
            pltpu.VMEM((3, nk), F32),
            pltpu.VMEM((1, 1), F32),
            pltpu.VMEM((SIDE, LANES), jnp.int32),
            pltpu.VMEM((144, nk), BF16),
            pltpu.VMEM((nk, 96), BF16),
            pltpu.VMEM((nk, 64), BF16),
            pltpu.VMEM((8, nk), F32),
            pltpu.VMEM((SIDE, HEAD_DIM, LANES), BF16),
            pltpu.VMEM((SIDE, HEAD_DIM, LANES), BF16),
            pltpu.VMEM((SIDE, 96, LANES), BF16),
            pltpu.VMEM((SIDE, 2, 8, LANES), F32),
            pltpu.VMEM((2 * SIDE, 2, 8, LANES), F32),
            pltpu.VMEM((SIDE, 8, LANES), F32),
            pltpu.VMEM((nk, 2 * LANES), F32),
            pltpu.VMEM((nk, 2 * LANES), BF16),
            pltpu.VMEM((SIDE // 2, nk, 2 * LANES), F32),
            pltpu.VMEM((2 * SIDE, 192, LANES), BF16),
            pltpu.VMEM((2 * SIDE, 8, LANES), F32),
            pltpu.VMEM((SIDE, 32, LANES), F32),
            pltpu.VMEM((SIDE, 32, LANES), F32),
            pltpu.VMEM((SIDE * SIDE, 16, LANES), BF16),
            pltpu.VMEM((4, 8, LANES), F32),
            pltpu.VMEM((2 * SIDE, 8, LANES), F32),
            pltpu.SemaphoreType.DMA((7,)),
            pltpu.SemaphoreType.DMA((10,)),
            pltpu.SemaphoreType.DMA((10,)),
        ],
        compiler_params=pltpu.CompilerParams(
            collective_id=0, has_side_effects=True, vmem_limit_bytes=60 * 1024 * 1024
        ),
    )(queries, keys, values, positions, falloff.reshape(1, 1), ids, cotangent)


def solution(mesh):
    return jax.shard_map(
        shards,
        mesh=mesh,
        in_specs=(
            P(None, "head"),
            P("head", "ctx"),
            P("head", "ctx"),
            P(None, "ctx"),
            P("head"),
            P(),
            P(None, "head"),
        ),
        out_specs=(P("head", None), P("head", None), P()),
        check_vma=False,
    )
```

```python
import functools

import jax
import jax.numpy as jnp
from jax import lax
from jax.experimental import pallas as pl
from jax.experimental.pallas import tpu as pltpu
from jax.sharding import PartitionSpec as P

MESH = pl.DeviceIdType.MESH
HEAD_DIM = 64
SIDE = 8
LANES = 128
CENTER = 2.0
F32 = jnp.float32
BF16 = jnp.bfloat16


def dot(a, b):
    return jnp.dot(a, b, preferred_element_type=F32)


def pieces(x, count):
    out = []
    for _ in range(count):
        part = x.astype(BF16).astype(F32)
        out.append(part)
        x = x - part
    return out


def rows(shape):
    return lax.broadcasted_iota(jnp.int32, shape, 0)


def total_of(terms):
    return functools.reduce(jnp.add, terms)


def weigh(stats):
    logs = [s[3:4] for s in stats]
    deltas = [s[7:8] for s in stats]
    top = functools.reduce(jnp.maximum, logs)
    weights = [jnp.exp(x - top) for x in logs]
    total = total_of(weights)
    inverse = 1.0 / total
    weights = [w * inverse for w in weights]
    delta = total_of([w * d for w, d in zip(weights, deltas)])
    shifts = [w * (d - delta) for w, d in zip(weights, deltas)]
    plain = total_of([w * s for w, s in zip(weights, stats)])
    moved = total_of([t * pltpu.roll(s, 4, 0) for t, s in zip(shifts, stats)])
    at = rows(plain.shape)
    stat = jnp.where(
        at < 3,
        plain + moved,
        jnp.where(at == 3, top + jnp.log(total), jnp.where(at < 7, plain, delta)),
    )
    return weights, shifts, stat


def combine(weights, shifts, parts):
    a = b = c = None
    for i, (w, t) in enumerate(zip(weights, shifts)):
        ai, bi, ci = parts(i)
        ai, bi, ci = w * ai, w * bi + t * ci, w * ci
        a, b, c = (ai, bi, ci) if a is None else (a + ai, b + bi, c + ci)
    return a, b, c


def kernel(
    q_hbm, k_hbm, v_hbm, pos_hbm, fall_hbm, ids_hbm, g_hbm,
    att_ref, qg_ref, f_ref,
    pos, pos2, fall, ids, left, kt, vt, xs, qin, gin, qx, pick1, sums, pick2, pick3, s_buf, p_buf,
    dp_buf, part_buf, stat_buf, stat2, sb2, rb2, gath, fin, fgath,
    local_sem, send, recv,
):
    h, ctx = lax.axis_index("head"), lax.axis_index("ctx")
    parity = h % 2
    mate = h + 1 - 2 * parity
    y, z = ctx // SIDE, ctx % SIDE
    m1, m2 = SIDE - (SIDE - 1) * parity, 1 + (SIDE - 1) * parity
    a1 = y + parity * (z - y)
    a2 = z + parity * (y - z)

    side = a1 % 2

    def on1(o):
        return ((a1 + o) % SIDE) * m1 + a2 * m2

    def on2(o):
        return a1 * m1 + ((a2 + o) % SIDE) * m2

    def far(k):
        return (SIDE // 2 + (1 - 2 * (k % 2)) * ((k + 1) // 2)) % SIDE

    def copy(phase, src, dst, dev):
        return pltpu.make_async_remote_copy(
            src_ref=src, dst_ref=dst, send_sem=send.at[phase],
            recv_sem=recv.at[phase], device_id=dev, device_id_type=MESH,
        )

    def loop(count, body):
        def step(o, carry):
            body(o)
            return carry
        lax.fori_loop(0, count, step, 0)

    def arrived(phase, ref):
        copy(phase, ref, ref, (h, ctx)).wait_recv()

    def sent(phase, ref):
        copy(phase, ref, ref, (h, ctx)).wait_send()

    def seven(ref):
        return ref.at[pl.ds(0, SIDE - 1)]

    key_count = k_hbm.shape[1]
    own_keys = pl.ds(0, key_count)
    other_keys = pl.ds(key_count, key_count)
    own_rows = pl.ds(pl.multiple_of(h * HEAD_DIM, HEAD_DIM), HEAD_DIM)
    loads = [
        pltpu.make_async_copy(src, dst, local_sem.at[i])
        for i, (src, dst) in enumerate([
            (pos_hbm, pos), (fall_hbm, fall), (ids_hbm, ids),
            (k_hbm, left.at[pl.ds(64, 64), own_keys]), (v_hbm, left.at[pl.ds(0, 64), own_keys]),
            (g_hbm.at[own_rows], gin.at[h]), (q_hbm.at[own_rows], qin.at[h]),
        ])
    ]
    for load in loads[:3]:
        load.start()

    barrier = pltpu.get_barrier_semaphore()

    def greet(head, at):
        pl.semaphore_signal(barrier, inc=1, device_id=(head, at), device_id_type=MESH)

    def greet_seven(k):
        o = far(k)
        greet(h, on1(o))
        greet(h, on2(o))
        greet((h + o) % SIDE, ctx)

    loop(SIDE - 1, greet_seven)
    loop(SIDE, lambda k: greet(mate, on1(far(k))))

    for load in loads[3:]:
        load.start()
    for load in loads[:3]:
        load.wait()
    falloff = fall[...]

    def key_side(ref, cols):
        place = ref[...] - CENTER
        xs[0:3, cols] = place
        xs[3:4, cols] = -falloff * jnp.sum(place * place, axis=0, keepdims=True)
        xs[4:7, cols] = place
        xs[7:8, cols] = jnp.ones((1, key_count), F32)
        x1, x2, x3 = pieces(xs[:, cols], 3)
        left[128:144, cols] = jnp.concatenate([x1, x2], axis=0).astype(BF16)
        return jnp.concatenate([x1, x2, x3, x1], axis=0).astype(BF16)

    keys_at = key_side(pos, own_keys)
    tiles = []
    for i in range(4):
        local = ids[pl.ds(4 * parity + i, 1), :] - ctx * key_count
        hot = (rows((key_count, LANES)) == local).astype(F32).astype(BF16)
        found = dot(keys_at[0:24], hot)
        tiles.append(found[0:8] + found[8:16] + found[16:24])
    low = rows(tiles[0].shape) < 4
    for i in range(2):
        pick1[a1, i] = jnp.where(low, tiles[i], tiles[i + 2])
    pl.semaphore_wait(barrier, 3 * (SIDE - 1) + SIDE)
    loop(SIDE - 1, lambda k: copy(0, pick1.at[a1], pick1.at[a1], (h, on1(far(k)))).start())

    def send_rows(ref_hbm, ref, phase):
        def body(k):
            other = (h + far(k)) % SIDE
            part = pl.ds(pl.multiple_of(other * HEAD_DIM, HEAD_DIM), HEAD_DIM)
            copy(phase, ref_hbm.at[part], ref.at[h], (other, ctx)).start()
        loop(SIDE - 1, body)

    partner = (h, (a1 + 1 - 2 * side) * m1 + a2 * m2)
    share_v = copy(12, v_hbm, left.at[pl.ds(0, 64), other_keys], partner)
    share_k = copy(13, k_hbm, left.at[pl.ds(64, 64), other_keys], partner)
    share_pos = copy(14, pos_hbm, pos2, partner)
    share_pos.start()
    share_v.start()
    share_k.start()
    send_rows(g_hbm, gin, 1)
    send_rows(q_hbm, qin, 2)
    for load in loads[3:]:
        load.wait()

    def turn(cols, at):
        kt[cols, :] = jnp.concatenate([left[64:128, cols], at], axis=0).T
        vt[cols, :] = left[0:64, cols].T

    turn(own_keys, keys_at)
    arrived(0, seven(pick1))
    for i in range(2):
        sums[i] = functools.reduce(jnp.add, [pick1[j, i] for j in range(SIDE)])
    slot2 = SIDE * parity + a2
    pick2[slot2] = sums[side]
    spread = pick2.at[slot2]
    loop(SIDE - 1, lambda k: copy(3, sums.at[side], spread, (h, on2(far(k)))).start())

    def send_mate(k):
        b = (a2 + far(k)) % SIDE
        copy(3, sums.at[b % 2], spread, (mate, a1 * m1 + b * m2)).start()

    loop(SIDE, send_mate)
    arrived(14, pos2)
    arrived(12, left.at[pl.ds(0, 64), other_keys])
    arrived(13, left.at[pl.ds(64, 64), other_keys])
    turn(other_keys, key_side(pos2, other_keys))
    arrived(1, seven(gin))

    def offsets(t):
        return [4 + 2 * t, 2 - 2 * t]

    def chunks(t):
        return [(a1 + o) % SIDE for o in offsets(t)]

    def grads(t):
        cot = jnp.concatenate([gin[c] for c in chunks(t)], axis=1)
        dp_buf[t] = dot(vt[...], cot)

    loop(2, grads)
    arrived(2, seven(qin))
    arrived(3, pick2.at[pl.ds(0, 2 * SIDE - 1)])
    for p in range(2):
        pair = functools.reduce(jnp.add, [pick2[SIDE * p + i] for i in range(SIDE)])
        low = rows(pair.shape) < 4
        swapped = pltpu.roll(pair, 4, 0)
        pick3[2 * p] = jnp.where(low, pair, swapped)
        pick3[2 * p + 1] = jnp.where(low, swapped, pair)

    def build(i):
        spot = pick3[i]
        at = rows(spot.shape)
        t = jnp.where(at < 3, (2.0 * falloff) * spot, jnp.where(at == 3, 1.0, 0.0))
        t1, t2 = pieces(t, 2)
        qx[i, 0:64, :] = qin[2 * i + side] * jnp.asarray(HEAD_DIM ** -0.5, BF16)
        qx[i, 64:96, :] = jnp.concatenate([t1, t1, t1, t2], axis=0).astype(BF16)

    loop(SIDE // 2, build)

    blocks = [pl.ds(i * 256, 256) for i in range(2 * key_count // 256)]

    place1 = a1 // 2
    three = pl.ds(0, 3)

    def attend(t):
        mine = chunks(t)
        q = jnp.concatenate([qx[c // 2] for c in mine], axis=1)
        cot = jnp.concatenate([gin[c] for c in mine], axis=1).astype(F32)
        top = None
        for part in blocks:
            s = dot(kt[part, :], q)
            s_buf[part, :] = s
            m = jnp.max(s, axis=0, keepdims=True)
            top = m if top is None else jnp.maximum(top, m)
        for part in blocks:
            p = jnp.exp(s_buf[part, :] - top)
            s_buf[part, :] = p
            p_buf[part, :] = p.astype(BF16)
        r = dot(left[...], p_buf[...])
        total = r[135:136]
        inverse = 1.0 / total
        a = r[0:64] * inverse
        c = r[64:128] * inverse
        px = (r[128:136] + r[136:144]) * inverse
        delta = jnp.sum(a * cot, axis=0, keepdims=True)
        places = []
        for i in range(2):
            o = offsets(t)[i]
            slot = jnp.where(o == 0, place1, SIDE // 2 + o // 2)
            lanes = slice(i * LANES, (i + 1) * LANES)
            places.append((o, slot, lanes))
            part_buf[slot, 0:64, :] = a[:, lanes].astype(BF16)
            part_buf[slot, 64:128, :] = c[:, lanes].astype(BF16)
            first = pl.ds(0, 128)

            @pl.when(o != 0)
            def _():
                copy(4, part_buf.at[slot, first], part_buf.at[place1, first], (h, on1(o))).start()

        for part in blocks:
            w = s_buf[part, :] * (dp_buf[t, part, :] - delta)
            p_buf[part, :] = w.astype(BF16)
        r = dot(left[64:144, :], p_buf[...])
        b = r[0:64] * inverse
        wx = (r[64:72] + r[72:80]) * inverse
        spot = jnp.concatenate([pick3[c // 2] for c in mine], axis=1)
        at = rows(spot.shape)
        stat = jnp.where(
            at < 3,
            wx - spot * wx[7:8],
            jnp.where(
                at == 3,
                top + jnp.log(total),
                jnp.where(at < 7, px - spot * px[7:8], delta),
            ),
        )
        for o, slot, lanes in places:
            stat_buf[slot] = stat[:, lanes]
            part_buf[slot, 128:192, :] = b[:, lanes].astype(BF16)
            last = pl.ds(128, 64)

            @pl.when(o != 0)
            def _():
                copy(5, stat_buf.at[slot], stat_buf.at[place1], (h, on1(o))).start()
                copy(10, part_buf.at[slot, last], part_buf.at[place1, last], (h, on1(o))).start()

    loop(2, attend)
    arrived(5, stat_buf.at[three])
    weights, shifts, stat = weigh([stat_buf[i] for i in range(SIDE // 2)])
    stat2[a2] = stat
    loop(SIDE - 1, lambda k: copy(11, stat2.at[a2], stat2.at[a2], (h, on2(far(k)))).start())
    arrived(4, part_buf.at[three, pl.ds(0, 128)])
    arrived(10, part_buf.at[three, pl.ds(128, 64)])
    def parts1(i):
        x = part_buf[i].astype(F32)
        return x[0:64], x[128:192], x[64:128]

    a, b, c = combine(weights, shifts, parts1)
    for j in range(SIDE):
        part = slice(8 * j, 8 * j + 8)
        sb2[j] = jnp.concatenate([a[part], b[part], c[part], c[part]], axis=0).astype(BF16)
    def send_second(k):
        o = far(k)
        copy(6, sb2.at[(a2 + o) % SIDE], rb2.at[a2], (h, on2(o))).start()

    loop(SIDE - 1, send_second)
    rb2[a2] = sb2[a2]
    arrived(11, seven(stat2))
    weights, shifts, stat = weigh([stat2[i] for i in range(SIDE)])
    fin[h // 2] = (2.0 * falloff) * stat

    def send_force(k):
        other = (h + 2 + 2 * k) % SIDE
        copy(7, fin.at[h // 2], fin.at[h // 2], (other, ctx)).start()

    loop(3, send_force)
    arrived(6, seven(rb2))
    def parts2(i):
        x = rb2[i].astype(F32)
        return x[0:8], x[8:16], x[16:24]

    a, b, c = combine(weights, shifts, parts2)
    tile = SIDE * a1 + a2
    gath[tile] = jnp.concatenate([a, b * HEAD_DIM ** -0.5], axis=0).astype(BF16)
    def send_tile(k):
        at = ((y + far(k % SIDE)) % SIDE) * SIDE + k // SIDE

        @pl.when(at != ctx)
        def _():
            copy(8, gath.at[tile], gath.at[tile], (h, at)).start()

    loop(SIDE * SIDE // 2, send_tile)
    arrived(7, fin.at[pl.ds(0, 3)])
    fgath[SIDE * parity + a1] = functools.reduce(jnp.add, [fin[i] for i in range(4)])
    ours = fgath.at[SIDE * parity + a1]
    loop(SIDE - 1, lambda k: copy(9, ours, ours, (h, on1(far(k)))).start())
    loop(SIDE, lambda k: copy(9, ours, ours, (mate, on1(far(k)))).start())
    loop(SIDE * SIDE // 2, lambda k: send_tile(k + SIDE * SIDE // 2))
    arrived(8, gath.at[pl.ds(0, SIDE * SIDE - 1)])
    for i in range(SIDE):
        lanes = slice(i * LANES, (i + 1) * LANES)
        for j in range(0, SIDE, 2):
            lo, hi = gath[SIDE * i + j].astype(F32), gath[SIDE * i + j + 1].astype(F32)
            att_ref[8 * j:8 * j + 16, lanes] = jnp.concatenate([lo[0:8], hi[0:8]], axis=0).astype(BF16)
            qg_ref[8 * j:8 * j + 8, lanes] = lo[8:16]
            qg_ref[8 * j + 8:8 * j + 16, lanes] = hi[8:16]
    arrived(9, fgath.at[pl.ds(0, 2 * SIDE - 1)])
    for i in range(SIDE):
        f_ref[:, i * LANES:(i + 1) * LANES] = fgath[i, 0:3, :] + fgath[SIDE + i, 0:3, :]
    sent(0, seven(pick1))
    sent(1, seven(gin))
    sent(2, seven(qin))
    sent(3, pick2.at[pl.ds(0, 2 * SIDE - 1)])
    sent(4, part_buf.at[three, pl.ds(0, 128)])
    sent(10, part_buf.at[three, pl.ds(128, 64)])
    sent(11, seven(stat2))
    sent(12, v_hbm)
    sent(13, k_hbm)
    sent(14, pos2)
    sent(5, stat_buf.at[three])
    sent(6, seven(rb2))
    sent(7, fin.at[pl.ds(0, 3)])
    sent(8, gath.at[pl.ds(0, SIDE * SIDE - 1)])
    sent(9, fgath.at[pl.ds(0, 2 * SIDE - 1)])


def shards(queries, keys, values, positions, falloff, query_ids, cotangent):
    nk = keys.shape[1]
    nq = query_ids.shape[0]
    ids = query_ids.reshape(SIDE, LANES)
    vmem = pl.BlockSpec(memory_space=pltpu.VMEM)
    any_ = pl.BlockSpec(memory_space=pl.ANY)
    return pl.pallas_call(
        kernel,
        out_shape=(
            pltpu.VMEM((HEAD_DIM, nq), BF16),
            pltpu.VMEM((HEAD_DIM, nq), F32),
            pltpu.VMEM((3, nq), F32),
        ),
        in_specs=[any_] * 7,
        out_specs=(vmem, vmem, vmem),
        scratch_shapes=[
            pltpu.VMEM((3, nk), F32),
            pltpu.VMEM((3, nk), F32),
            pltpu.VMEM((1, 1), F32),
            pltpu.VMEM((SIDE, LANES), jnp.int32),
            pltpu.VMEM((144, 2 * nk), BF16),
            pltpu.VMEM((2 * nk, 96), BF16),
            pltpu.VMEM((2 * nk, 64), BF16),
            pltpu.VMEM((8, 2 * nk), F32),
            pltpu.VMEM((SIDE, HEAD_DIM, LANES), BF16),
            pltpu.VMEM((SIDE, HEAD_DIM, LANES), BF16),
            pltpu.VMEM((SIDE // 2, 96, LANES), BF16),
            pltpu.VMEM((SIDE, 2, 8, LANES), F32),
            pltpu.VMEM((2, 8, LANES), F32),
            pltpu.VMEM((2 * SIDE, 8, LANES), F32),
            pltpu.VMEM((SIDE // 2, 8, LANES), F32),
            pltpu.VMEM((2 * nk, 2 * LANES), F32),
            pltpu.VMEM((2 * nk, 2 * LANES), BF16),
            pltpu.VMEM((SIDE // 4, 2 * nk, 2 * LANES), F32),
            pltpu.VMEM((SIDE, 192, LANES), BF16),
            pltpu.VMEM((SIDE, 8, LANES), F32),
            pltpu.VMEM((SIDE, 8, LANES), F32),
            pltpu.VMEM((SIDE, 32, LANES), BF16),
            pltpu.VMEM((SIDE, 32, LANES), BF16),
            pltpu.VMEM((SIDE * SIDE, 16, LANES), BF16),
            pltpu.VMEM((4, 8, LANES), F32),
            pltpu.VMEM((2 * SIDE, 8, LANES), F32),
            pltpu.SemaphoreType.DMA((7,)),
            pltpu.SemaphoreType.DMA((15,)),
            pltpu.SemaphoreType.DMA((15,)),
        ],
        compiler_params=pltpu.CompilerParams(
            collective_id=0, has_side_effects=True, vmem_limit_bytes=56 * 1024 * 1024
        ),
    )(queries, keys, values, positions, falloff.reshape(1, 1), ids, cotangent)


def solution(mesh):
    return jax.shard_map(
        shards,
        mesh=mesh,
        in_specs=(
            P(None, "head"),
            P("head", "ctx"),
            P("head", "ctx"),
            P(None, "ctx"),
            P("head"),
            P(),
            P(None, "head"),
        ),
        out_specs=(P("head", None), P("head", None), P()),
        check_vma=False,
    )
```

```python
import functools

import jax
import jax.numpy as jnp
from jax import lax
from jax.experimental import pallas as pl
from jax.experimental.pallas import tpu as pltpu
from jax.sharding import PartitionSpec as P

MESH = pl.DeviceIdType.MESH
HEAD_DIM = 64
SIDE = 8
LANES = 128
CENTER = 2.0
F32 = jnp.float32
BF16 = jnp.bfloat16


def dot(a, b):
    return jnp.dot(a, b, preferred_element_type=F32)


def pieces(x, count):
    out = []
    for _ in range(count):
        part = x.astype(BF16).astype(F32)
        out.append(part)
        x = x - part
    return out


def rows(shape):
    return lax.broadcasted_iota(jnp.int32, shape, 0)


def total_of(terms):
    return functools.reduce(jnp.add, terms)


def weigh(stats):
    logs = [s[3:4] for s in stats]
    deltas = [s[7:8] for s in stats]
    top = functools.reduce(jnp.maximum, logs)
    weights = [jnp.exp(x - top) for x in logs]
    total = total_of(weights)
    inverse = 1.0 / total
    weights = [w * inverse for w in weights]
    delta = total_of([w * d for w, d in zip(weights, deltas)])
    shifts = [w * (d - delta) for w, d in zip(weights, deltas)]
    plain = total_of([w * s for w, s in zip(weights, stats)])
    moved = total_of([t * pltpu.roll(s, 4, 0) for t, s in zip(shifts, stats)])
    at = rows(plain.shape)
    stat = jnp.where(
        at < 3,
        plain + moved,
        jnp.where(at == 3, top + jnp.log(total), jnp.where(at < 7, plain, delta)),
    )
    return weights, shifts, stat


def combine(weights, shifts, parts):
    a = b = c = None
    for i, (w, t) in enumerate(zip(weights, shifts)):
        ai, bi, ci = parts(i)
        ai, bi, ci = w * ai, w * bi + t * ci, w * ci
        a, b, c = (ai, bi, ci) if a is None else (a + ai, b + bi, c + ci)
    return a, b, c


def kernel(
    q_hbm, k_hbm, v_hbm, pos_hbm, fall_hbm, ids_hbm, g_hbm,
    att_ref, qg_ref, f_ref,
    pos, pos2, fall, ids, left, kt, vt, xs, qin, gin, qx, pick1, sums, pick2, pick3, s_buf, p_buf,
    dp_buf, part_buf, stat_buf, stat2, sb2, rb2, gath, fin, fgath,
    local_sem, send, recv,
):
    h, ctx = lax.axis_index("head"), lax.axis_index("ctx")
    parity = h % 2
    mate = h + 1 - 2 * parity
    y, z = ctx // SIDE, ctx % SIDE
    m1, m2 = SIDE - (SIDE - 1) * parity, 1 + (SIDE - 1) * parity
    a1 = y + parity * (z - y)
    a2 = z + parity * (y - z)

    side = a1 % 2

    def on1(o):
        return ((a1 + o) % SIDE) * m1 + a2 * m2

    def on2(o):
        return a1 * m1 + ((a2 + o) % SIDE) * m2

    def far(k):
        return (SIDE // 2 + (1 - 2 * (k % 2)) * ((k + 1) // 2)) % SIDE

    def copy(phase, src, dst, dev):
        return pltpu.make_async_remote_copy(
            src_ref=src, dst_ref=dst, send_sem=send.at[phase],
            recv_sem=recv.at[phase], device_id=dev, device_id_type=MESH,
        )

    def loop(count, body):
        def step(o, carry):
            body(o)
            return carry
        lax.fori_loop(0, count, step, 0)

    def arrived(phase, ref):
        copy(phase, ref, ref, (h, ctx)).wait_recv()

    def sent(phase, ref):
        copy(phase, ref, ref, (h, ctx)).wait_send()

    def seven(ref):
        return ref.at[pl.ds(0, SIDE - 1)]

    key_count = k_hbm.shape[1]
    own_keys = pl.ds(0, key_count)
    other_keys = pl.ds(key_count, key_count)
    own_rows = pl.ds(pl.multiple_of(h * HEAD_DIM, HEAD_DIM), HEAD_DIM)
    loads = [
        pltpu.make_async_copy(src, dst, local_sem.at[i])
        for i, (src, dst) in enumerate([
            (pos_hbm, pos), (fall_hbm, fall), (ids_hbm, ids),
            (k_hbm, left.at[pl.ds(64, 64), own_keys]), (v_hbm, left.at[pl.ds(0, 64), own_keys]),
            (g_hbm.at[own_rows], gin.at[h]), (q_hbm.at[own_rows], qin.at[h]),
        ])
    ]
    for load in loads[:3]:
        load.start()

    barrier = pltpu.get_barrier_semaphore()

    def greet(head, at):
        pl.semaphore_signal(barrier, inc=1, device_id=(head, at), device_id_type=MESH)

    def greet_seven(k):
        o = far(k)
        greet(h, on1(o))
        greet(h, on2(o))
        greet((h + o) % SIDE, ctx)

    loop(SIDE - 1, greet_seven)
    loop(SIDE, lambda k: greet(mate, on1(far(k))))

    for load in loads[3:]:
        load.start()
    for load in loads[:3]:
        load.wait()
    falloff = fall[...]

    def key_side(ref, cols):
        place = ref[...] - CENTER
        xs[0:3, cols] = place
        xs[3:4, cols] = -falloff * jnp.sum(place * place, axis=0, keepdims=True)
        xs[4:7, cols] = place
        xs[7:8, cols] = jnp.ones((1, key_count), F32)
        x1, x2, x3 = pieces(xs[:, cols], 3)
        left[128:144, cols] = jnp.concatenate([x1, x2], axis=0).astype(BF16)
        return jnp.concatenate([x1, x2, x3, x1], axis=0).astype(BF16)

    keys_at = key_side(pos, own_keys)
    tiles = []
    for i in range(4):
        local = ids[pl.ds(4 * parity + i, 1), :] - ctx * key_count
        hot = (rows((key_count, LANES)) == local).astype(F32).astype(BF16)
        found = dot(keys_at[0:24], hot)
        tiles.append(found[0:8] + found[8:16] + found[16:24])
    low = rows(tiles[0].shape) < 4
    for i in range(2):
        pick1[a1, i] = jnp.where(low, tiles[i], tiles[i + 2])
    pl.semaphore_wait(barrier, 3 * (SIDE - 1) + SIDE)
    loop(SIDE - 1, lambda k: copy(0, pick1.at[a1], pick1.at[a1], (h, on1(far(k)))).start())

    def send_rows(ref_hbm, ref, phase):
        def body(k):
            other = (h + far(k)) % SIDE
            part = pl.ds(pl.multiple_of(other * HEAD_DIM, HEAD_DIM), HEAD_DIM)
            copy(phase, ref_hbm.at[part], ref.at[h], (other, ctx)).start()
        loop(SIDE - 1, body)

    partner = (h, (a1 + 1 - 2 * side) * m1 + a2 * m2)
    share_v = copy(12, v_hbm, left.at[pl.ds(0, 64), other_keys], partner)
    share_k = copy(13, k_hbm, left.at[pl.ds(64, 64), other_keys], partner)
    share_pos = copy(14, pos_hbm, pos2, partner)
    share_pos.start()
    share_v.start()
    share_k.start()
    send_rows(g_hbm, gin, 1)
    send_rows(q_hbm, qin, 2)
    for load in loads[3:]:
        load.wait()

    def turn(cols, at):
        kt[cols, :] = jnp.concatenate([left[64:128, cols], at], axis=0).T
        vt[cols, :] = left[0:64, cols].T

    turn(own_keys, keys_at)
    arrived(0, seven(pick1))
    for i in range(2):
        sums[i] = functools.reduce(jnp.add, [pick1[j, i] for j in range(SIDE)])
    slot2 = SIDE * parity + a2
    pick2[slot2] = sums[side]
    spread = pick2.at[slot2]
    loop(SIDE - 1, lambda k: copy(3, sums.at[side], spread, (h, on2(far(k)))).start())

    def send_mate(k):
        b = (a2 + far(k)) % SIDE
        copy(3, sums.at[b % 2], spread, (mate, a1 * m1 + b * m2)).start()

    loop(SIDE, send_mate)
    arrived(14, pos2)
    arrived(12, left.at[pl.ds(0, 64), other_keys])
    arrived(13, left.at[pl.ds(64, 64), other_keys])
    turn(other_keys, key_side(pos2, other_keys))
    arrived(1, seven(gin))

    def offsets(t):
        return [4 + 2 * t, 2 - 2 * t]

    def chunks(t):
        return [(a1 + o) % SIDE for o in offsets(t)]

    def grads(t):
        cot = jnp.concatenate([gin[c] for c in chunks(t)], axis=1)
        dp_buf[t] = dot(vt[...], cot)

    loop(2, grads)
    arrived(2, seven(qin))
    arrived(3, pick2.at[pl.ds(0, 2 * SIDE - 1)])
    for p in range(2):
        pair = functools.reduce(jnp.add, [pick2[SIDE * p + i] for i in range(SIDE)])
        low = rows(pair.shape) < 4
        swapped = pltpu.roll(pair, 4, 0)
        pick3[2 * p] = jnp.where(low, pair, swapped)
        pick3[2 * p + 1] = jnp.where(low, swapped, pair)

    def build(i):
        spot = pick3[i]
        at = rows(spot.shape)
        t = jnp.where(at < 3, (2.0 * falloff) * spot, jnp.where(at == 3, 1.0, 0.0))
        t1, t2 = pieces(t, 2)
        qx[i, 0:64, :] = qin[2 * i + side] * jnp.asarray(HEAD_DIM ** -0.5, BF16)
        qx[i, 64:96, :] = jnp.concatenate([t1, t1, t1, t2], axis=0).astype(BF16)

    loop(SIDE // 2, build)

    blocks = [pl.ds(i * 256, 256) for i in range(2 * key_count // 256)]

    place1 = a1 // 2
    three = pl.ds(0, 3)

    def attend(t):
        mine = chunks(t)
        q = jnp.concatenate([qx[c // 2] for c in mine], axis=1)
        cot = jnp.concatenate([gin[c] for c in mine], axis=1).astype(F32)
        top = None
        for part in blocks:
            s = dot(kt[part, :], q)
            s_buf[part, :] = s
            m = jnp.max(s, axis=0, keepdims=True)
            top = m if top is None else jnp.maximum(top, m)
        for part in blocks:
            p = jnp.exp(s_buf[part, :] - top)
            s_buf[part, :] = p
            p_buf[part, :] = p.astype(BF16)
        r = dot(left[...], p_buf[...])
        total = r[135:136]
        inverse = 1.0 / total
        a = r[0:64] * inverse
        c = r[64:128] * inverse
        px = (r[128:136] + r[136:144]) * inverse
        delta = jnp.sum(a * cot, axis=0, keepdims=True)
        places = []
        for i in range(2):
            o = offsets(t)[i]
            slot = jnp.where(o == 0, place1, SIDE // 2 + o // 2)
            lanes = slice(i * LANES, (i + 1) * LANES)
            places.append((o, slot, lanes))
            part_buf[slot, 0:64, :] = a[:, lanes].astype(BF16)
            part_buf[slot, 64:128, :] = c[:, lanes].astype(BF16)
            first = pl.ds(0, 128)

            @pl.when(o != 0)
            def _():
                copy(4, part_buf.at[slot, first], part_buf.at[place1, first], (h, on1(o))).start()

        for part in blocks:
            w = s_buf[part, :] * (dp_buf[t, part, :] - delta)
            p_buf[part, :] = w.astype(BF16)
        r = dot(left[64:144, :], p_buf[...])
        b = r[0:64] * inverse
        wx = (r[64:72] + r[72:80]) * inverse
        spot = jnp.concatenate([pick3[c // 2] for c in mine], axis=1)
        at = rows(spot.shape)
        stat = jnp.where(
            at < 3,
            wx - spot * wx[7:8],
            jnp.where(
                at == 3,
                top + jnp.log(total),
                jnp.where(at < 7, px - spot * px[7:8], delta),
            ),
        )
        for o, slot, lanes in places:
            stat_buf[slot] = stat[:, lanes]
            part_buf[slot, 128:192, :] = b[:, lanes].astype(BF16)
            last = pl.ds(128, 64)

            @pl.when(o != 0)
            def _():
                copy(5, stat_buf.at[slot], stat_buf.at[place1], (h, on1(o))).start()
                copy(10, part_buf.at[slot, last], part_buf.at[place1, last], (h, on1(o))).start()

    loop(2, attend)
    arrived(5, stat_buf.at[three])
    weights, shifts, stat = weigh([stat_buf[i] for i in range(SIDE // 2)])
    stat2[a2] = stat
    loop(SIDE - 1, lambda k: copy(11, stat2.at[a2], stat2.at[a2], (h, on2(far(k)))).start())
    arrived(4, part_buf.at[three, pl.ds(0, 128)])
    arrived(10, part_buf.at[three, pl.ds(128, 64)])
    def parts1(i):
        x = part_buf[i].astype(F32)
        return x[0:64], x[128:192], x[64:128]

    a, b, c = combine(weights, shifts, parts1)
    for j in range(SIDE):
        part = slice(8 * j, 8 * j + 8)
        sb2[j] = jnp.concatenate([a[part], b[part], c[part], c[part]], axis=0).astype(BF16)
    def send_second(k):
        o = far(k)
        copy(6, sb2.at[(a2 + o) % SIDE], rb2.at[a2], (h, on2(o))).start()

    loop(SIDE - 1, send_second)
    rb2[a2] = sb2[a2]
    arrived(11, seven(stat2))
    weights, shifts, stat = weigh([stat2[i] for i in range(SIDE)])
    fin[h // 2] = (2.0 * falloff) * stat

    def send_force(k):
        other = (h + 2 + 2 * k) % SIDE
        copy(7, fin.at[h // 2], fin.at[h // 2], (other, ctx)).start()

    loop(3, send_force)
    arrived(6, seven(rb2))
    def parts2(i):
        x = rb2[i].astype(F32)
        return x[0:8], x[8:16], x[16:24]

    a, b, c = combine(weights, shifts, parts2)
    tile = SIDE * a1 + a2
    gath[tile] = jnp.concatenate([a, b * HEAD_DIM ** -0.5], axis=0).astype(BF16)
    def send_tile(k):
        at = ((y + far(k % SIDE)) % SIDE) * SIDE + k // SIDE

        @pl.when(at != ctx)
        def _():
            copy(8, gath.at[tile], gath.at[tile], (h, at)).start()

    loop(SIDE * SIDE // 2, send_tile)
    arrived(7, fin.at[pl.ds(0, 3)])
    fgath[SIDE * parity + a1] = functools.reduce(jnp.add, [fin[i] for i in range(4)])
    ours = fgath.at[SIDE * parity + a1]
    loop(SIDE - 1, lambda k: copy(9, ours, ours, (h, on1(far(k)))).start())
    loop(SIDE, lambda k: copy(9, ours, ours, (mate, on1(far(k)))).start())
    loop(SIDE * SIDE // 2, lambda k: send_tile(k + SIDE * SIDE // 2))
    arrived(8, gath.at[pl.ds(0, SIDE * SIDE - 1)])
    for i in range(SIDE):
        lanes = slice(i * LANES, (i + 1) * LANES)
        for j in range(0, SIDE, 2):
            lo, hi = gath[SIDE * i + j].astype(F32), gath[SIDE * i + j + 1].astype(F32)
            att_ref[8 * j:8 * j + 16, lanes] = jnp.concatenate([lo[0:8], hi[0:8]], axis=0).astype(BF16)
            qg_ref[8 * j:8 * j + 8, lanes] = lo[8:16]
            qg_ref[8 * j + 8:8 * j + 16, lanes] = hi[8:16]
    arrived(9, fgath.at[pl.ds(0, 2 * SIDE - 1)])
    for i in range(SIDE):
        f_ref[:, i * LANES:(i + 1) * LANES] = fgath[i, 0:3, :] + fgath[SIDE + i, 0:3, :]
    sent(0, seven(pick1))
    sent(1, seven(gin))
    sent(2, seven(qin))
    sent(3, pick2.at[pl.ds(0, 2 * SIDE - 1)])
    sent(4, part_buf.at[three, pl.ds(0, 128)])
    sent(10, part_buf.at[three, pl.ds(128, 64)])
    sent(11, seven(stat2))
    sent(12, v_hbm)
    sent(13, k_hbm)
    sent(14, pos2)
    sent(5, stat_buf.at[three])
    sent(6, seven(rb2))
    sent(7, fin.at[pl.ds(0, 3)])
    sent(8, gath.at[pl.ds(0, SIDE * SIDE - 1)])
    sent(9, fgath.at[pl.ds(0, 2 * SIDE - 1)])


def store(*refs):
    sems = refs[6]
    copies = [pltpu.make_async_copy(refs[i], refs[3 + i], sems.at[i]) for i in range(3)]
    for c in copies:
        c.start()
    for c in copies:
        c.wait()


def shards(queries, keys, values, positions, falloff, query_ids, cotangent):
    nk = keys.shape[1]
    nq = query_ids.shape[0]
    ids = query_ids.reshape(SIDE, LANES)
    vmem = pl.BlockSpec(memory_space=pltpu.VMEM)
    any_ = pl.BlockSpec(memory_space=pl.ANY)
    results = pl.pallas_call(
        kernel,
        out_shape=(
            pltpu.VMEM((HEAD_DIM, nq), BF16),
            pltpu.VMEM((HEAD_DIM, nq), F32),
            pltpu.VMEM((3, nq), F32),
        ),
        in_specs=[any_] * 7,
        out_specs=(vmem, vmem, vmem),
        scratch_shapes=[
            pltpu.VMEM((3, nk), F32),
            pltpu.VMEM((3, nk), F32),
            pltpu.VMEM((1, 1), F32),
            pltpu.VMEM((SIDE, LANES), jnp.int32),
            pltpu.VMEM((144, 2 * nk), BF16),
            pltpu.VMEM((2 * nk, 96), BF16),
            pltpu.VMEM((2 * nk, 64), BF16),
            pltpu.VMEM((8, 2 * nk), F32),
            pltpu.VMEM((SIDE, HEAD_DIM, LANES), BF16),
            pltpu.VMEM((SIDE, HEAD_DIM, LANES), BF16),
            pltpu.VMEM((SIDE // 2, 96, LANES), BF16),
            pltpu.VMEM((SIDE, 2, 8, LANES), F32),
            pltpu.VMEM((2, 8, LANES), F32),
            pltpu.VMEM((2 * SIDE, 8, LANES), F32),
            pltpu.VMEM((SIDE // 2, 8, LANES), F32),
            pltpu.VMEM((2 * nk, 2 * LANES), F32),
            pltpu.VMEM((2 * nk, 2 * LANES), BF16),
            pltpu.VMEM((SIDE // 4, 2 * nk, 2 * LANES), F32),
            pltpu.VMEM((SIDE, 192, LANES), BF16),
            pltpu.VMEM((SIDE, 8, LANES), F32),
            pltpu.VMEM((SIDE, 8, LANES), F32),
            pltpu.VMEM((SIDE, 32, LANES), BF16),
            pltpu.VMEM((SIDE, 32, LANES), BF16),
            pltpu.VMEM((SIDE * SIDE, 16, LANES), BF16),
            pltpu.VMEM((4, 8, LANES), F32),
            pltpu.VMEM((2 * SIDE, 8, LANES), F32),
            pltpu.SemaphoreType.DMA((7,)),
            pltpu.SemaphoreType.DMA((15,)),
            pltpu.SemaphoreType.DMA((15,)),
        ],
        compiler_params=pltpu.CompilerParams(
            collective_id=0, has_side_effects=True, vmem_limit_bytes=56 * 1024 * 1024
        ),
    )(queries, keys, values, positions, falloff.reshape(1, 1), ids, cotangent)
    return pl.pallas_call(
        store,
        out_shape=tuple(jax.ShapeDtypeStruct(x.shape, x.dtype) for x in results),
        in_specs=[any_] * 3,
        out_specs=(any_, any_, any_),
        scratch_shapes=[pltpu.SemaphoreType.DMA((3,))],
        compiler_params=pltpu.CompilerParams(vmem_limit_bytes=8 * 1024 * 1024),
    )(*results)


def solution(mesh):
    return jax.shard_map(
        shards,
        mesh=mesh,
        in_specs=(
            P(None, "head"),
            P("head", "ctx"),
            P("head", "ctx"),
            P(None, "ctx"),
            P("head"),
            P(),
            P(None, "head"),
        ),
        out_specs=(P("head", None), P("head", None), P()),
        check_vma=False,
    )
```

```python
import functools

import jax
import jax.numpy as jnp
from jax import lax
from jax.experimental import pallas as pl
from jax.experimental.pallas import tpu as pltpu
from jax.sharding import PartitionSpec as P

MESH = pl.DeviceIdType.MESH
HEAD_DIM = 64
SIDE = 8
LANES = 128
CENTER = 2.0
F32 = jnp.float32
BF16 = jnp.bfloat16


def dot(a, b):
    return jnp.dot(a, b, preferred_element_type=F32)


def pieces(x, count):
    out = []
    for _ in range(count):
        part = x.astype(BF16).astype(F32)
        out.append(part)
        x = x - part
    return out


def rows(shape):
    return lax.broadcasted_iota(jnp.int32, shape, 0)


def total_of(terms):
    return functools.reduce(jnp.add, terms)


def weigh(stats):
    logs = [s[3:4] for s in stats]
    deltas = [s[7:8] for s in stats]
    top = functools.reduce(jnp.maximum, logs)
    weights = [jnp.exp(x - top) for x in logs]
    total = total_of(weights)
    inverse = 1.0 / total
    weights = [w * inverse for w in weights]
    delta = total_of([w * d for w, d in zip(weights, deltas)])
    shifts = [w * (d - delta) for w, d in zip(weights, deltas)]
    plain = total_of([w * s for w, s in zip(weights, stats)])
    moved = total_of([t * pltpu.roll(s, 4, 0) for t, s in zip(shifts, stats)])
    at = rows(plain.shape)
    stat = jnp.where(
        at < 3,
        plain + moved,
        jnp.where(at == 3, top + jnp.log(total), jnp.where(at < 7, plain, delta)),
    )
    return weights, shifts, stat


def combine(weights, shifts, parts):
    a = b = c = None
    for i, (w, t) in enumerate(zip(weights, shifts)):
        ai, bi, ci = parts(i)
        ai, bi, ci = w * ai, w * bi + t * ci, w * ci
        a, b, c = (ai, bi, ci) if a is None else (a + ai, b + bi, c + ci)
    return a, b, c


def kernel(
    q_hbm, k_hbm, v_hbm, pos_hbm, fall_hbm, ids_hbm, g_hbm,
    att_ref, qg_ref, f_ref,
    pos, pos2, fall, ids, left, kt, vt, xs, qin, gin, qx, pick1, sums, pick2, pick3, s_buf, p_buf,
    dp_buf, part_buf, stat_buf, stat2, sb2, rb2, gath, fgath,
    local_sem, send, recv,
):
    h, ctx = lax.axis_index("head"), lax.axis_index("ctx")
    parity = h % 2
    mate = h + 1 - 2 * parity
    y, z = ctx // SIDE, ctx % SIDE
    m1, m2 = SIDE - (SIDE - 1) * parity, 1 + (SIDE - 1) * parity
    a1 = y + parity * (z - y)
    a2 = z + parity * (y - z)

    side, place1 = a1 % 2, a1 // 2
    three = pl.ds(0, 3)

    def on1(o):
        return ((a1 + o) % SIDE) * m1 + a2 * m2

    def on2(o):
        return a1 * m1 + ((a2 + o) % SIDE) * m2

    def far(k):
        return (SIDE // 2 + (1 - 2 * (k % 2)) * ((k + 1) // 2)) % SIDE

    def copy(phase, src, dst, dev):
        return pltpu.make_async_remote_copy(
            src_ref=src, dst_ref=dst, send_sem=send.at[phase],
            recv_sem=recv.at[phase], device_id=dev, device_id_type=MESH,
        )

    def loop(count, body):
        def step(o, carry):
            body(o)
            return carry
        lax.fori_loop(0, count, step, 0)

    def arrived(phase, ref):
        copy(phase, ref, ref, (h, ctx)).wait_recv()

    def sent(phase, ref):
        copy(phase, ref, ref, (h, ctx)).wait_send()

    def seven(ref):
        return ref.at[pl.ds(0, SIDE - 1)]

    key_count = k_hbm.shape[1]
    own_keys = pl.ds(0, key_count)
    other_keys = pl.ds(key_count, key_count)
    own_rows = pl.ds(pl.multiple_of(h * HEAD_DIM, HEAD_DIM), HEAD_DIM)
    loads = [
        pltpu.make_async_copy(src, dst, local_sem.at[i])
        for i, (src, dst) in enumerate([
            (pos_hbm, pos), (fall_hbm, fall), (ids_hbm, ids),
            (k_hbm, left.at[pl.ds(64, 64), own_keys]), (v_hbm, left.at[pl.ds(0, 64), own_keys]),
            (g_hbm.at[own_rows], gin.at[h]), (q_hbm.at[own_rows], qin.at[h]),
        ])
    ]
    for load in loads[:3]:
        load.start()

    barrier = pltpu.get_barrier_semaphore()

    def greet(head, at):
        pl.semaphore_signal(barrier, inc=1, device_id=(head, at), device_id_type=MESH)

    def greet_seven(k):
        o = far(k)
        greet(h, on1(o))
        greet(h, on2(o))
        greet((h + o) % SIDE, ctx)

    loop(SIDE - 1, greet_seven)
    loop(SIDE, lambda k: greet(mate, on1(far(k))))

    for load in loads[3:]:
        load.start()
    for load in loads[:3]:
        load.wait()
    falloff = fall[...]

    def key_side(ref, cols):
        place = ref[...] - CENTER
        xs[0:3, cols] = place
        xs[3:4, cols] = -falloff * jnp.sum(place * place, axis=0, keepdims=True)
        xs[4:7, cols] = place
        xs[7:8, cols] = jnp.ones((1, key_count), F32)
        x1, x2, x3 = pieces(xs[:, cols], 3)
        left[128:144, cols] = jnp.concatenate([x1, x2], axis=0).astype(BF16)
        return jnp.concatenate([x1, x2, x3, x1], axis=0).astype(BF16)

    keys_at = key_side(pos, own_keys)
    tiles = []
    for i in range(4):
        local = ids[pl.ds(4 * parity + i, 1), :] - ctx * key_count
        hot = (rows((key_count, LANES)) == local).astype(F32).astype(BF16)
        found = dot(keys_at[0:24], hot)
        tiles.append(found[0:8] + found[8:16] + found[16:24])
    low = rows(tiles[0].shape) < 4
    for i in range(2):
        pick1[a1, i] = jnp.where(low, tiles[i], tiles[i + 2])
    pl.semaphore_wait(barrier, 3 * (SIDE - 1) + SIDE)
    loop(SIDE - 1, lambda k: copy(0, pick1.at[a1], pick1.at[a1], (h, on1(far(k)))).start())

    def send_rows(ref_hbm, ref, phase):
        def body(k):
            other = (h + far(k)) % SIDE
            part = pl.ds(pl.multiple_of(other * HEAD_DIM, HEAD_DIM), HEAD_DIM)
            copy(phase, ref_hbm.at[part], ref.at[h], (other, ctx)).start()
        loop(SIDE - 1, body)

    partner = (h, (a1 + 1 - 2 * side) * m1 + a2 * m2)
    share_v = copy(12, v_hbm, left.at[pl.ds(0, 64), other_keys], partner)
    share_k = copy(13, k_hbm, left.at[pl.ds(64, 64), other_keys], partner)
    share_pos = copy(14, pos_hbm, pos2, partner)
    share_pos.start()
    share_v.start()
    share_k.start()
    send_rows(g_hbm, gin, 1)
    send_rows(q_hbm, qin, 2)
    for load in loads[3:]:
        load.wait()

    def turn(cols, at):
        kt[cols, :] = jnp.concatenate([left[64:128, cols], at], axis=0).T
        vt[cols, :] = left[0:64, cols].T

    turn(own_keys, keys_at)
    arrived(0, seven(pick1))
    for i in range(2):
        sums[i] = functools.reduce(jnp.add, [pick1[j, i] for j in range(SIDE)])
    slot2 = SIDE * parity + a2
    pick2[slot2] = sums[side]
    spread = pick2.at[slot2]
    loop(SIDE - 1, lambda k: copy(3, sums.at[side], spread, (h, on2(far(k)))).start())

    def send_mate(k):
        b = (a2 + far(k)) % SIDE
        copy(3, sums.at[b % 2], spread, (mate, a1 * m1 + b * m2)).start()

    loop(SIDE, send_mate)
    arrived(14, pos2)
    arrived(12, left.at[pl.ds(0, 64), other_keys])
    arrived(13, left.at[pl.ds(64, 64), other_keys])
    turn(other_keys, key_side(pos2, other_keys))
    arrived(1, seven(gin))

    def offsets(t):
        return [4 + 2 * t, 2 - 2 * t]

    def chunks(t):
        return [(a1 + o) % SIDE for o in offsets(t)]

    def grads(t):
        cot = jnp.concatenate([gin[c] for c in chunks(t)], axis=1)
        dp_buf[t] = dot(vt[...], cot)

    loop(2, grads)
    arrived(2, seven(qin))
    arrived(3, pick2.at[pl.ds(0, 2 * SIDE - 1)])
    for p in range(2):
        pair = functools.reduce(jnp.add, [pick2[SIDE * p + i] for i in range(SIDE)])
        low = rows(pair.shape) < 4
        swapped = pltpu.roll(pair, 4, 0)
        pick3[2 * p] = jnp.where(low, pair, swapped)
        pick3[2 * p + 1] = jnp.where(low, swapped, pair)

    def build(i):
        spot = pick3[i]
        at = rows(spot.shape)
        t = jnp.where(at < 3, (2.0 * falloff) * spot, jnp.where(at == 3, 1.0, 0.0))
        t1, t2 = pieces(t, 2)
        qx[i, 0:64, :] = qin[2 * i + side] * jnp.asarray(HEAD_DIM ** -0.5, BF16)
        qx[i, 64:96, :] = jnp.concatenate([t1, t1, t1, t2], axis=0).astype(BF16)

    loop(SIDE // 2, build)

    blocks = [pl.ds(i * 256, 256) for i in range(2 * key_count // 256)]

    def attend(t):
        mine = chunks(t)
        q = jnp.concatenate([qx[c // 2] for c in mine], axis=1)
        cot = jnp.concatenate([gin[c] for c in mine], axis=1).astype(F32)
        top = None
        for part in blocks:
            s = dot(kt[part, :], q)
            s_buf[part, :] = s
            m = jnp.max(s, axis=0, keepdims=True)
            top = m if top is None else jnp.maximum(top, m)
        for part in blocks:
            p = jnp.exp(s_buf[part, :] - top)
            s_buf[part, :] = p
            p_buf[part, :] = p.astype(BF16)
        r = dot(left[...], p_buf[...])
        total = r[135:136]
        inverse = 1.0 / total
        a = r[0:64] * inverse
        c = r[64:128] * inverse
        px = (r[128:136] + r[136:144]) * inverse
        delta = jnp.sum(a * cot, axis=0, keepdims=True)
        places = []
        for i in range(2):
            o = offsets(t)[i]
            slot = jnp.where(o == 0, place1, SIDE // 2 + o // 2)
            lanes = slice(i * LANES, (i + 1) * LANES)
            places.append((o, slot, lanes))
            part_buf[slot, 0:64, :] = a[:, lanes].astype(BF16)
            part_buf[slot, 64:128, :] = c[:, lanes].astype(BF16)
            first = pl.ds(0, 128)

            @pl.when(o != 0)
            def _():
                copy(4, part_buf.at[slot, first], part_buf.at[place1, first], (h, on1(o))).start()

        for part in blocks:
            w = s_buf[part, :] * (dp_buf[t, part, :] - delta)
            p_buf[part, :] = w.astype(BF16)
        r = dot(left[64:144, :], p_buf[...])
        b = r[0:64] * inverse
        wx = (r[64:72] + r[72:80]) * inverse
        spot = jnp.concatenate([pick3[c // 2] for c in mine], axis=1)
        at = rows(spot.shape)
        stat = jnp.where(
            at < 3,
            (2.0 * falloff) * (wx - spot * wx[7:8]),
            jnp.where(
                at == 3,
                top + jnp.log(total),
                jnp.where(at < 7, (2.0 * falloff) * (px - spot * px[7:8]), delta),
            ),
        )
        for o, slot, lanes in places:
            stat_buf[slot] = stat[:, lanes]
            part_buf[slot, 128:192, :] = b[:, lanes].astype(BF16)
            last = pl.ds(128, 64)

            @pl.when(o != 0)
            def _():
                copy(5, stat_buf.at[slot], stat_buf.at[place1], (h, on1(o))).start()
                copy(10, part_buf.at[slot, last], part_buf.at[place1, last], (h, on1(o))).start()

    loop(2, attend)
    arrived(5, stat_buf.at[three])
    weights, shifts, stat = weigh([stat_buf[i] for i in range(SIDE // 2)])
    own = SIDE * (h // 2) + a2
    stat2[own] = stat
    ours2 = stat2.at[own]
    loop(SIDE - 1, lambda k: copy(11, ours2, ours2, (h, on2(far(k)))).start())

    def send_others(k):
        other = (h + 2 + 2 * (k // SIDE)) % SIDE
        copy(7, ours2, ours2, (other, on2(far(k % SIDE)))).start()

    arrived(4, part_buf.at[three, pl.ds(0, 128)])
    arrived(10, part_buf.at[three, pl.ds(128, 64)])
    def parts1(i):
        x = part_buf[i].astype(F32)
        return x[0:64], x[128:192], x[64:128]

    a, b, c = combine(weights, shifts, parts1)
    for j in range(SIDE):
        part = slice(8 * j, 8 * j + 8)
        sb2[j] = jnp.concatenate([a[part], b[part], c[part], c[part]], axis=0).astype(BF16)
    def send_second(k):
        o = far(k)
        copy(6, sb2.at[(a2 + o) % SIDE], rb2.at[a2], (h, on2(o))).start()

    loop(SIDE - 1, send_second)
    loop(3 * SIDE, send_others)
    rb2[a2] = sb2[a2]
    arrived(11, seven(stat2))
    weights, shifts, _ = weigh([stat2[SIDE * (h // 2) + i] for i in range(SIDE)])
    arrived(6, seven(rb2))
    def parts2(i):
        x = rb2[i].astype(F32)
        return x[0:8], x[8:16], x[16:24]

    a, b, c = combine(weights, shifts, parts2)
    tile = SIDE * a1 + a2
    gath[tile] = jnp.concatenate([a, b * HEAD_DIM ** -0.5], axis=0).astype(BF16)
    def send_tile(k):
        at = ((y + far(k % SIDE)) % SIDE) * SIDE + k // SIDE

        @pl.when(at != ctx)
        def _():
            copy(8, gath.at[tile], gath.at[tile], (h, at)).start()

    loop(SIDE * SIDE // 2, send_tile)
    arrived(7, stat2.at[pl.ds(0, 3 * SIDE)])
    fgath[SIDE * parity + a1] = total_of(
        [weigh([stat2[SIDE * i + j] for j in range(SIDE)])[2] for i in range(4)]
    )
    ours = fgath.at[SIDE * parity + a1]
    loop(SIDE - 1, lambda k: copy(9, ours, ours, (h, on1(far(k)))).start())
    loop(SIDE, lambda k: copy(9, ours, ours, (mate, on1(far(k)))).start())
    loop(SIDE * SIDE // 2, lambda k: send_tile(k + SIDE * SIDE // 2))
    arrived(8, gath.at[pl.ds(0, SIDE * SIDE - 1)])
    for i in range(SIDE):
        lanes = slice(i * LANES, (i + 1) * LANES)
        for j in range(0, SIDE, 2):
            lo, hi = gath[SIDE * i + j].astype(F32), gath[SIDE * i + j + 1].astype(F32)
            att_ref[8 * j:8 * j + 16, lanes] = jnp.concatenate([lo[0:8], hi[0:8]], axis=0).astype(BF16)
            qg_ref[8 * j:8 * j + 8, lanes] = lo[8:16]
            qg_ref[8 * j + 8:8 * j + 16, lanes] = hi[8:16]
    arrived(9, fgath.at[pl.ds(0, 2 * SIDE - 1)])
    for i in range(SIDE):
        f_ref[:, i * LANES:(i + 1) * LANES] = fgath[i, 0:3, :] + fgath[SIDE + i, 0:3, :]
    sent(0, seven(pick1))
    sent(1, seven(gin))
    sent(2, seven(qin))
    sent(3, pick2.at[pl.ds(0, 2 * SIDE - 1)])
    sent(4, part_buf.at[three, pl.ds(0, 128)])
    sent(10, part_buf.at[three, pl.ds(128, 64)])
    sent(11, seven(stat2))
    sent(12, v_hbm)
    sent(13, k_hbm)
    sent(14, pos2)
    sent(5, stat_buf.at[three])
    sent(6, seven(rb2))
    sent(7, stat2.at[pl.ds(0, 3 * SIDE)])
    sent(8, gath.at[pl.ds(0, SIDE * SIDE - 1)])
    sent(9, fgath.at[pl.ds(0, 2 * SIDE - 1)])


def store(*refs):
    sems = refs[6]
    copies = [pltpu.make_async_copy(refs[i], refs[3 + i], sems.at[i]) for i in range(3)]
    for c in copies:
        c.start()
    for c in copies:
        c.wait()


def shards(queries, keys, values, positions, falloff, query_ids, cotangent):
    nk = keys.shape[1]
    nq = query_ids.shape[0]
    ids = query_ids.reshape(SIDE, LANES)
    vmem = pl.BlockSpec(memory_space=pltpu.VMEM)
    any_ = pl.BlockSpec(memory_space=pl.ANY)
    results = pl.pallas_call(
        kernel,
        out_shape=(
            pltpu.VMEM((HEAD_DIM, nq), BF16),
            pltpu.VMEM((HEAD_DIM, nq), F32),
            pltpu.VMEM((3, nq), F32),
        ),
        in_specs=[any_] * 7,
        out_specs=(vmem, vmem, vmem),
        scratch_shapes=[
            pltpu.VMEM((3, nk), F32),
            pltpu.VMEM((3, nk), F32),
            pltpu.VMEM((1, 1), F32),
            pltpu.VMEM((SIDE, LANES), jnp.int32),
            pltpu.VMEM((144, 2 * nk), BF16),
            pltpu.VMEM((2 * nk, 96), BF16),
            pltpu.VMEM((2 * nk, 64), BF16),
            pltpu.VMEM((8, 2 * nk), F32),
            pltpu.VMEM((SIDE, HEAD_DIM, LANES), BF16),
            pltpu.VMEM((SIDE, HEAD_DIM, LANES), BF16),
            pltpu.VMEM((SIDE // 2, 96, LANES), BF16),
            pltpu.VMEM((SIDE, 2, 8, LANES), F32),
            pltpu.VMEM((2, 8, LANES), F32),
            pltpu.VMEM((2 * SIDE, 8, LANES), F32),
            pltpu.VMEM((SIDE // 2, 8, LANES), F32),
            pltpu.VMEM((2 * nk, 2 * LANES), F32),
            pltpu.VMEM((2 * nk, 2 * LANES), BF16),
            pltpu.VMEM((SIDE // 4, 2 * nk, 2 * LANES), F32),
            pltpu.VMEM((SIDE, 192, LANES), BF16),
            pltpu.VMEM((SIDE, 8, LANES), F32),
            pltpu.VMEM((4 * SIDE, 8, LANES), F32),
            pltpu.VMEM((SIDE, 32, LANES), BF16),
            pltpu.VMEM((SIDE, 32, LANES), BF16),
            pltpu.VMEM((SIDE * SIDE, 16, LANES), BF16),
            pltpu.VMEM((2 * SIDE, 8, LANES), F32),
            pltpu.SemaphoreType.DMA((7,)),
            pltpu.SemaphoreType.DMA((15,)),
            pltpu.SemaphoreType.DMA((15,)),
        ],
        compiler_params=pltpu.CompilerParams(
            collective_id=0, has_side_effects=True, vmem_limit_bytes=56 * 1024 * 1024
        ),
    )(queries, keys, values, positions, falloff.reshape(1, 1), ids, cotangent)
    return pl.pallas_call(
        store,
        out_shape=tuple(jax.ShapeDtypeStruct(x.shape, x.dtype) for x in results),
        in_specs=[any_] * 3,
        out_specs=(any_, any_, any_),
        scratch_shapes=[pltpu.SemaphoreType.DMA((3,))],
        compiler_params=pltpu.CompilerParams(vmem_limit_bytes=8 * 1024 * 1024),
    )(*results)


def solution(mesh):
    return jax.shard_map(
        shards,
        mesh=mesh,
        in_specs=(
            P(None, "head"),
            P("head", "ctx"),
            P("head", "ctx"),
            P(None, "ctx"),
            P("head"),
            P(),
            P(None, "head"),
        ),
        out_specs=(P("head", None), P("head", None), P()),
        check_vma=False,
    )
```

```python
import functools

import jax
import jax.numpy as jnp
from jax import lax
from jax.experimental import pallas as pl
from jax.experimental.pallas import tpu as pltpu
from jax.sharding import PartitionSpec as P

MESH = pl.DeviceIdType.MESH
HEAD_DIM = 64
SIDE = 8
LANES = 128
CENTER = 2.0
F32 = jnp.float32
BF16 = jnp.bfloat16


def dot(a, b):
    return jnp.dot(a, b, preferred_element_type=F32)


def pieces(x, count):
    out = []
    for _ in range(count):
        part = x.astype(BF16).astype(F32)
        out.append(part)
        x = x - part
    return out


def rows(shape):
    return lax.broadcasted_iota(jnp.int32, shape, 0)


def total_of(terms):
    return functools.reduce(jnp.add, terms)


def weigh(stats):
    logs = [s[3:4] for s in stats]
    deltas = [s[7:8] for s in stats]
    top = functools.reduce(jnp.maximum, logs)
    weights = [jnp.exp(x - top) for x in logs]
    total = total_of(weights)
    inverse = 1.0 / total
    weights = [w * inverse for w in weights]
    delta = total_of([w * d for w, d in zip(weights, deltas)])
    shifts = [w * (d - delta) for w, d in zip(weights, deltas)]
    plain = total_of([w * s for w, s in zip(weights, stats)])
    moved = total_of([t * pltpu.roll(s, 4, 0) for t, s in zip(shifts, stats)])
    at = rows(plain.shape)
    stat = jnp.where(
        at < 3,
        plain + moved,
        jnp.where(at == 3, top + jnp.log(total), jnp.where(at < 7, plain, delta)),
    )
    return weights, shifts, stat


def combine(weights, shifts, parts):
    a = b = c = None
    for i, (w, t) in enumerate(zip(weights, shifts)):
        ai, bi, ci = parts(i)
        ai, bi, ci = w * ai, w * bi + t * ci, w * ci
        a, b, c = (ai, bi, ci) if a is None else (a + ai, b + bi, c + ci)
    return a, b, c


def kernel(
    q_hbm, k_hbm, v_hbm, pos_hbm, fall_hbm, ids_hbm, g_hbm,
    att_ref, qg_ref, f_ref,
    pos, pos2, fall, ids, left, kt, vt, xs, qin, gin, qx, pick1, sums, pick2, pick3, s_buf, p_buf,
    dp_buf, part_buf, stat_buf, stat2, sb2, rb2, gath, fgath,
    local_sem, send, recv,
):
    h, ctx = lax.axis_index("head"), lax.axis_index("ctx")
    parity = h % 2
    mate = h + 1 - 2 * parity
    y, z = ctx // SIDE, ctx % SIDE
    m1, m2 = SIDE - (SIDE - 1) * parity, 1 + (SIDE - 1) * parity
    a1 = y + parity * (z - y)
    a2 = z + parity * (y - z)

    side, place1 = a1 % 2, a1 // 2
    three = pl.ds(0, 3)

    def on1(o):
        return ((a1 + o) % SIDE) * m1 + a2 * m2

    def on2(o):
        return a1 * m1 + ((a2 + o) % SIDE) * m2

    def far(k):
        return (SIDE // 2 + (1 - 2 * (k % 2)) * ((k + 1) // 2)) % SIDE

    def copy(phase, src, dst, dev):
        return pltpu.make_async_remote_copy(
            src_ref=src, dst_ref=dst, send_sem=send.at[phase],
            recv_sem=recv.at[phase], device_id=dev, device_id_type=MESH,
        )

    def loop(count, body):
        def step(o, carry):
            body(o)
            return carry
        lax.fori_loop(0, count, step, 0)

    def arrived(phase, ref):
        copy(phase, ref, ref, (h, ctx)).wait_recv()

    def sent(phase, ref):
        copy(phase, ref, ref, (h, ctx)).wait_send()

    def seven(ref):
        return ref.at[pl.ds(0, SIDE - 1)]

    key_count = k_hbm.shape[1]
    own_keys = pl.ds(0, key_count)
    other_keys = pl.ds(key_count, key_count)
    own_rows = pl.ds(pl.multiple_of(h * HEAD_DIM, HEAD_DIM), HEAD_DIM)
    loads = [
        pltpu.make_async_copy(src, dst, local_sem.at[i])
        for i, (src, dst) in enumerate([
            (pos_hbm, pos), (fall_hbm, fall), (ids_hbm, ids),
            (k_hbm, left.at[pl.ds(64, 64), own_keys]), (v_hbm, left.at[pl.ds(0, 64), own_keys]),
            (g_hbm.at[own_rows], gin.at[h]), (q_hbm.at[own_rows], qin.at[h]),
        ])
    ]
    for load in loads[:3]:
        load.start()

    barrier = pltpu.get_barrier_semaphore()

    def greet(head, at):
        pl.semaphore_signal(barrier, inc=1, device_id=(head, at), device_id_type=MESH)

    def greet_seven(k):
        o = far(k)
        greet(h, on1(o))
        greet(h, on2(o))
        greet((h + o) % SIDE, ctx)

    loop(SIDE - 1, greet_seven)
    loop(SIDE, lambda k: greet(mate, on1(far(k))))

    for load in loads[3:]:
        load.start()
    for load in loads[:3]:
        load.wait()
    falloff = fall[...]

    def key_side(ref, cols):
        place = ref[...] - CENTER
        xs[0:3, cols] = place
        xs[3:4, cols] = -falloff * jnp.sum(place * place, axis=0, keepdims=True)
        xs[4:7, cols] = place
        xs[7:8, cols] = jnp.ones((1, key_count), F32)
        x1, x2, x3 = pieces(xs[:, cols], 3)
        left[128:144, cols] = jnp.concatenate([x1, x2], axis=0).astype(BF16)
        return jnp.concatenate([x1, x2, x3, x1], axis=0).astype(BF16)

    keys_at = key_side(pos, own_keys)
    tiles = []
    for i in range(4):
        local = ids[pl.ds(4 * parity + i, 1), :] - ctx * key_count
        hot = (rows((key_count, LANES)) == local).astype(F32).astype(BF16)
        found = dot(keys_at[0:24], hot)
        tiles.append(found[0:8] + found[8:16] + found[16:24])
    low = rows(tiles[0].shape) < 4
    for i in range(2):
        pick1[a1, i] = jnp.where(low, tiles[i], tiles[i + 2])
    pl.semaphore_wait(barrier, 3 * (SIDE - 1) + SIDE)
    loop(SIDE - 1, lambda k: copy(0, pick1.at[a1], pick1.at[a1], (h, on1(far(k)))).start())

    def uses(other):
        return (h + y + (other % 2) * (z - y)) % 2 == 0

    def blocks_arrived(phase, ref):
        @pl.when((h + a1) % 2 == 0)
        def _():
            arrived(phase, ref.at[pl.ds(0, SIDE // 2 - 1)])

        @pl.when((h + a1) % 2 != 0)
        def _():
            arrived(phase, ref.at[pl.ds(0, SIDE // 2)])

    def blocks_sent(phase, ref):
        def body(k):
            @pl.when(uses((h + far(k)) % SIDE))
            def _():
                sent(phase, ref.at[0])
        loop(SIDE - 1, body)

    def send_rows(ref_hbm, ref, phase):
        def body(k):
            other = (h + far(k)) % SIDE
            part = pl.ds(pl.multiple_of(other * HEAD_DIM, HEAD_DIM), HEAD_DIM)

            @pl.when(uses(other))
            def _():
                copy(phase, ref_hbm.at[part], ref.at[h], (other, ctx)).start()
        loop(SIDE - 1, body)

    partner = (h, (a1 + 1 - 2 * side) * m1 + a2 * m2)
    share_v = copy(12, v_hbm, left.at[pl.ds(0, 64), other_keys], partner)
    share_k = copy(13, k_hbm, left.at[pl.ds(64, 64), other_keys], partner)
    share_pos = copy(14, pos_hbm, pos2, partner)
    share_pos.start()
    share_v.start()
    share_k.start()
    send_rows(g_hbm, gin, 1)
    send_rows(q_hbm, qin, 2)
    for load in loads[3:]:
        load.wait()

    def turn(cols, at):
        kt[cols, :] = jnp.concatenate([left[64:128, cols], at], axis=0).T
        vt[cols, :] = left[0:64, cols].T

    turn(own_keys, keys_at)
    arrived(0, seven(pick1))
    for i in range(2):
        sums[i] = functools.reduce(jnp.add, [pick1[j, i] for j in range(SIDE)])
    slot2 = SIDE * parity + a2
    pick2[slot2] = sums[side]
    spread = pick2.at[slot2]
    loop(SIDE - 1, lambda k: copy(3, sums.at[side], spread, (h, on2(far(k)))).start())

    def send_mate(k):
        b = (a2 + far(k)) % SIDE
        copy(3, sums.at[b % 2], spread, (mate, a1 * m1 + b * m2)).start()

    loop(SIDE, send_mate)
    arrived(14, pos2)
    arrived(12, left.at[pl.ds(0, 64), other_keys])
    arrived(13, left.at[pl.ds(64, 64), other_keys])
    turn(other_keys, key_side(pos2, other_keys))
    blocks_arrived(1, gin)

    def offsets(t):
        return [4 + 2 * t, 2 - 2 * t]

    def chunks(t):
        return [(a1 + o) % SIDE for o in offsets(t)]

    def grads(t):
        cot = jnp.concatenate([gin[c] for c in chunks(t)], axis=1)
        dp_buf[t] = dot(vt[...], cot)

    loop(2, grads)
    blocks_arrived(2, qin)
    arrived(3, pick2.at[pl.ds(0, 2 * SIDE - 1)])
    for p in range(2):
        pair = functools.reduce(jnp.add, [pick2[SIDE * p + i] for i in range(SIDE)])
        low = rows(pair.shape) < 4
        swapped = pltpu.roll(pair, 4, 0)
        pick3[2 * p] = jnp.where(low, pair, swapped)
        pick3[2 * p + 1] = jnp.where(low, swapped, pair)

    def build(i):
        spot = pick3[i]
        at = rows(spot.shape)
        t = jnp.where(at < 3, (2.0 * falloff) * spot, jnp.where(at == 3, 1.0, 0.0))
        t1, t2 = pieces(t, 2)
        qx[i, 0:64, :] = qin[2 * i + side] * jnp.asarray(HEAD_DIM ** -0.5, BF16)
        qx[i, 64:96, :] = jnp.concatenate([t1, t1, t1, t2], axis=0).astype(BF16)

    loop(SIDE // 2, build)

    blocks = [pl.ds(i * 256, 256) for i in range(2 * key_count // 256)]

    def attend(t):
        mine = chunks(t)
        q = jnp.concatenate([qx[c // 2] for c in mine], axis=1)
        cot = jnp.concatenate([gin[c] for c in mine], axis=1).astype(F32)
        top = None
        for part in blocks:
            s = dot(kt[part, :], q)
            s_buf[part, :] = s
            m = jnp.max(s, axis=0, keepdims=True)
            top = m if top is None else jnp.maximum(top, m)
        for part in blocks:
            p = jnp.exp(s_buf[part, :] - top)
            s_buf[part, :] = p
            p_buf[part, :] = p.astype(BF16)
        r = dot(left[...], p_buf[...])
        total = r[135:136]
        inverse = 1.0 / total
        a = r[0:64] * inverse
        c = r[64:128] * inverse
        px = (r[128:136] + r[136:144]) * inverse
        delta = jnp.sum(a * cot, axis=0, keepdims=True)
        places = []
        for i in range(2):
            o = offsets(t)[i]
            slot = jnp.where(o == 0, place1, SIDE // 2 + o // 2)
            lanes = slice(i * LANES, (i + 1) * LANES)
            places.append((o, slot, lanes))
            part_buf[slot, 0:64, :] = a[:, lanes].astype(BF16)
            part_buf[slot, 64:128, :] = c[:, lanes].astype(BF16)
            first = pl.ds(0, 128)

            @pl.when(o != 0)
            def _():
                copy(4, part_buf.at[slot, first], part_buf.at[place1, first], (h, on1(o))).start()

        for part in blocks:
            w = s_buf[part, :] * (dp_buf[t, part, :] - delta)
            p_buf[part, :] = w.astype(BF16)
        r = dot(left[64:144, :], p_buf[...])
        b = r[0:64] * inverse
        wx = (r[64:72] + r[72:80]) * inverse
        spot = jnp.concatenate([pick3[c // 2] for c in mine], axis=1)
        at = rows(spot.shape)
        stat = jnp.where(
            at < 3,
            (2.0 * falloff) * (wx - spot * wx[7:8]),
            jnp.where(
                at == 3,
                top + jnp.log(total),
                jnp.where(at < 7, (2.0 * falloff) * (px - spot * px[7:8]), delta),
            ),
        )
        for o, slot, lanes in places:
            stat_buf[slot] = stat[:, lanes]
            part_buf[slot, 128:192, :] = b[:, lanes].astype(BF16)
            last = pl.ds(128, 64)

            @pl.when(o != 0)
            def _():
                copy(5, stat_buf.at[slot], stat_buf.at[place1], (h, on1(o))).start()
                copy(10, part_buf.at[slot, last], part_buf.at[place1, last], (h, on1(o))).start()

    loop(2, attend)
    arrived(5, stat_buf.at[three])
    weights, shifts, stat = weigh([stat_buf[i] for i in range(SIDE // 2)])
    own = SIDE * (h // 2) + a2
    stat2[own] = stat
    ours2 = stat2.at[own]
    loop(SIDE - 1, lambda k: copy(11, ours2, ours2, (h, on2(far(k)))).start())

    def send_others(k):
        other = (h + 2 + 2 * (k // SIDE)) % SIDE
        copy(7, ours2, ours2, (other, on2(far(k % SIDE)))).start()

    arrived(4, part_buf.at[three, pl.ds(0, 128)])
    arrived(10, part_buf.at[three, pl.ds(128, 64)])
    def parts1(i):
        x = part_buf[i].astype(F32)
        return x[0:64], x[128:192], x[64:128]

    a, b, c = combine(weights, shifts, parts1)
    for j in range(SIDE):
        part = slice(8 * j, 8 * j + 8)
        sb2[j] = jnp.concatenate([a[part], b[part], c[part], c[part]], axis=0).astype(BF16)
    def send_second(k):
        o = far(k)
        copy(6, sb2.at[(a2 + o) % SIDE], rb2.at[a2], (h, on2(o))).start()

    loop(SIDE - 1, send_second)
    loop(3 * SIDE, send_others)
    rb2[a2] = sb2[a2]
    arrived(11, seven(stat2))
    weights, shifts, _ = weigh([stat2[SIDE * (h // 2) + i] for i in range(SIDE)])
    arrived(6, seven(rb2))
    def parts2(i):
        x = rb2[i].astype(F32)
        return x[0:8], x[8:16], x[16:24]

    a, b, c = combine(weights, shifts, parts2)
    tile = SIDE * a1 + a2
    gath[tile] = jnp.concatenate([a, b * HEAD_DIM ** -0.5], axis=0).astype(BF16)
    def send_tile(k):
        at = ((y + far(k % SIDE)) % SIDE) * SIDE + k // SIDE

        @pl.when(at != ctx)
        def _():
            copy(8, gath.at[tile], gath.at[tile], (h, at)).start()

    loop(SIDE * SIDE // 2, send_tile)
    arrived(7, stat2.at[pl.ds(0, 3 * SIDE)])
    fgath[SIDE * parity + a1] = total_of(
        [weigh([stat2[SIDE * i + j] for j in range(SIDE)])[2] for i in range(4)]
    )
    ours = fgath.at[SIDE * parity + a1]
    loop(SIDE - 1, lambda k: copy(9, ours, ours, (h, on1(far(k)))).start())
    loop(SIDE, lambda k: copy(9, ours, ours, (mate, on1(far(k)))).start())
    loop(SIDE * SIDE // 2, lambda k: send_tile(k + SIDE * SIDE // 2))
    arrived(8, gath.at[pl.ds(0, SIDE * SIDE - 1)])
    for i in range(SIDE):
        lanes = slice(i * LANES, (i + 1) * LANES)
        for j in range(0, SIDE, 2):
            lo, hi = gath[SIDE * i + j].astype(F32), gath[SIDE * i + j + 1].astype(F32)
            att_ref[8 * j:8 * j + 16, lanes] = jnp.concatenate([lo[0:8], hi[0:8]], axis=0).astype(BF16)
            qg_ref[8 * j:8 * j + 8, lanes] = lo[8:16]
            qg_ref[8 * j + 8:8 * j + 16, lanes] = hi[8:16]
    arrived(9, fgath.at[pl.ds(0, 2 * SIDE - 1)])
    for i in range(SIDE):
        f_ref[:, i * LANES:(i + 1) * LANES] = fgath[i, 0:3, :] + fgath[SIDE + i, 0:3, :]
    sent(0, seven(pick1))
    blocks_sent(1, gin)
    blocks_sent(2, qin)
    sent(3, pick2.at[pl.ds(0, 2 * SIDE - 1)])
    sent(4, part_buf.at[three, pl.ds(0, 128)])
    sent(10, part_buf.at[three, pl.ds(128, 64)])
    sent(11, seven(stat2))
    sent(12, v_hbm)
    sent(13, k_hbm)
    sent(14, pos2)
    sent(5, stat_buf.at[three])
    sent(6, seven(rb2))
    sent(7, stat2.at[pl.ds(0, 3 * SIDE)])
    sent(8, gath.at[pl.ds(0, SIDE * SIDE - 1)])
    sent(9, fgath.at[pl.ds(0, 2 * SIDE - 1)])


def store(*refs):
    sems = refs[6]
    copies = [pltpu.make_async_copy(refs[i], refs[3 + i], sems.at[i]) for i in range(3)]
    for c in copies:
        c.start()
    for c in copies:
        c.wait()


def shards(queries, keys, values, positions, falloff, query_ids, cotangent):
    nk = keys.shape[1]
    nq = query_ids.shape[0]
    ids = query_ids.reshape(SIDE, LANES)
    vmem = pl.BlockSpec(memory_space=pltpu.VMEM)
    any_ = pl.BlockSpec(memory_space=pl.ANY)
    results = pl.pallas_call(
        kernel,
        out_shape=(
            pltpu.VMEM((HEAD_DIM, nq), BF16),
            pltpu.VMEM((HEAD_DIM, nq), F32),
            pltpu.VMEM((3, nq), F32),
        ),
        in_specs=[any_] * 7,
        out_specs=(vmem, vmem, vmem),
        scratch_shapes=[
            pltpu.VMEM((3, nk), F32),
            pltpu.VMEM((3, nk), F32),
            pltpu.VMEM((1, 1), F32),
            pltpu.VMEM((SIDE, LANES), jnp.int32),
            pltpu.VMEM((144, 2 * nk), BF16),
            pltpu.VMEM((2 * nk, 96), BF16),
            pltpu.VMEM((2 * nk, 64), BF16),
            pltpu.VMEM((8, 2 * nk), F32),
            pltpu.VMEM((SIDE, HEAD_DIM, LANES), BF16),
            pltpu.VMEM((SIDE, HEAD_DIM, LANES), BF16),
            pltpu.VMEM((SIDE // 2, 96, LANES), BF16),
            pltpu.VMEM((SIDE, 2, 8, LANES), F32),
            pltpu.VMEM((2, 8, LANES), F32),
            pltpu.VMEM((2 * SIDE, 8, LANES), F32),
            pltpu.VMEM((SIDE // 2, 8, LANES), F32),
            pltpu.VMEM((2 * nk, 2 * LANES), F32),
            pltpu.VMEM((2 * nk, 2 * LANES), BF16),
            pltpu.VMEM((SIDE // 4, 2 * nk, 2 * LANES), F32),
            pltpu.VMEM((SIDE, 192, LANES), BF16),
            pltpu.VMEM((SIDE, 8, LANES), F32),
            pltpu.VMEM((4 * SIDE, 8, LANES), F32),
            pltpu.VMEM((SIDE, 32, LANES), BF16),
            pltpu.VMEM((SIDE, 32, LANES), BF16),
            pltpu.VMEM((SIDE * SIDE, 16, LANES), BF16),
            pltpu.VMEM((2 * SIDE, 8, LANES), F32),
            pltpu.SemaphoreType.DMA((7,)),
            pltpu.SemaphoreType.DMA((15,)),
            pltpu.SemaphoreType.DMA((15,)),
        ],
        compiler_params=pltpu.CompilerParams(
            collective_id=0, has_side_effects=True, vmem_limit_bytes=56 * 1024 * 1024
        ),
    )(queries, keys, values, positions, falloff.reshape(1, 1), ids, cotangent)
    return pl.pallas_call(
        store,
        out_shape=tuple(jax.ShapeDtypeStruct(x.shape, x.dtype) for x in results),
        in_specs=[any_] * 3,
        out_specs=(any_, any_, any_),
        scratch_shapes=[pltpu.SemaphoreType.DMA((3,))],
        compiler_params=pltpu.CompilerParams(vmem_limit_bytes=8 * 1024 * 1024),
    )(*results)


def solution(mesh):
    return jax.shard_map(
        shards,
        mesh=mesh,
        in_specs=(
            P(None, "head"),
            P("head", "ctx"),
            P("head", "ctx"),
            P(None, "ctx"),
            P("head"),
            P(),
            P(None, "head"),
        ),
        out_specs=(P("head", None), P("head", None), P()),
        check_vma=False,
    )
```
